1024 devices in a mesh: row: 8 (over z_lo), col: 16 (over y, z_hi), depth: 8 (over x, core).
Axes of the slice: x: 4, y: 8, z: 16 (z_hi: 2, z_lo: 8; z = z_hi * 8 + z_lo), core: 2. Of those that a mesh axis runs over, the one named last changes fastest.
Arguments:
- grad_out: bfloat16 [32768, 1024], P(('col', 'row')), may hold values from -6 to 6
- relu_mask: int32 [32768, 1024], P(('col', 'row')), may hold values 0 or 1
- aggregated: bfloat16 [32768, 1024], P(('col', 'row'), 'depth'), may hold values from -0.03125 to 0.03125
- weight: bfloat16 [1024, 1024], P('depth'), may hold values from -0.1875 to 0.1875
- adj_tiles: bfloat16 [8, 16, 160, 128, 128], P('row', 'col'), may hold values from -0.078125 to 0.078125
- tile_row: int32 [8, 16, 160], P('row', 'col'), may hold values from 0 to 31
- tile_col: int32 [8, 16, 160], P('row', 'col'), may hold values from 0 to 15
- tile_count: int32 [8, 16], P('row', 'col'), may hold values from 20 to 160, as said below
Outputs:
- grad_features: bfloat16 [32768, 1024], P(('row', 'col'), 'depth')
- grad_weight: float32 [1024, 1024], P('depth')
The draws below stay inside these ranges and needn't reach their ends.
Inputs may be any that keep to these rules, and one draw needn't show every extreme that they name: `tile_count`: some block has all 160 slots live.
All inputs are finite; a program needn't handle non-finite values. No bound on the sum of `relu_mask` on one device may be relied on, other than what follows from the above.
Results may differ from the reference program's by a relative error of at most 0.018.
Values may be sent and summed in bfloat16 or wider, within the bound.
No kernel may reach another device: no remote copies, remote signals or barrier semaphores. Data moves between devices by JAX's collectives and lax.ppermute only.
A program may use at most 64 MiB of HBM per device.

```python
import jax
import jax.numpy as jnp
from jax import lax

FIN = 1024
FOUT = 1024
TILE = 128
NODES_DEV = 256
TILES_DEV = 160
NODES = 32768
N_ROW = 8
N_COL = 16


def draw_tile_count(key, part):
    key = jax.random.fold_in(key, 7)
    key_shift, key_busy = jax.random.split(key)
    shifts = jax.random.randint(key_shift, (N_ROW * N_COL,), 0, 4)
    counts = jnp.right_shift(jnp.full((N_ROW * N_COL,), TILES_DEV, jnp.int32), shifts.astype(jnp.int32))
    busiest = jax.random.randint(key_busy, (), 0, N_ROW * N_COL)
    counts = jnp.where(jnp.arange(N_ROW * N_COL) == busiest, TILES_DEV, counts)
    return counts.reshape(N_ROW, N_COL).astype(jnp.int32)


def with_ends(result, own_key, smallest, top_value):
    extent = result.shape
    place = [jax.random.randint(jax.random.fold_in(own_key, axis), (), 0, extent[axis]) for axis in range(len(extent))]
    result = result.at[tuple(place)].set(smallest)
    longest = extent.index(max(extent))
    place[longest] = (place[longest] + 1) % extent[longest]
    return result.at[tuple(place)].set(top_value)


def block_levels(key, shape, pieces, low, top_value):
    def one(axis_at, shards_of):
        steps = jax.random.uniform(jax.random.fold_in(jax.random.fold_in(key, 6), axis_at), (shards_of,), jnp.float32, low / len(pieces), top_value / len(pieces))
        return jnp.repeat(jnp.exp(steps), shape[axis_at] // shards_of).reshape((-1,) + (1,) * (len(shape) - axis_at - 1))

    gain = one(*pieces[0])
    for cut in pieces[1:]:
        gain = gain * one(*cut)
    return gain


def gaussian(key, extent, deviation, most, shards=(), kind=jnp.bfloat16):
    drawn = deviation * jax.random.normal(key, extent, jnp.float32)
    if shards:
        drawn = drawn * block_levels(key, extent, shards, -0.22, 0.18)
    return jnp.clip(drawn, -most, most).astype(kind)


def setup_inputs(seed: int = 0) -> dict:
    seeds = jax.random.split(jax.random.key(seed), 9)
    return {
        "grad_out": gaussian(seeds[0], (NODES, FOUT), 1.0, 6.0, ((0, 128),)),
        "relu_mask": with_ends((jax.random.randint(seeds[1], (NODES, FOUT), 0, 2) < 1).astype(jnp.int32), jax.random.fold_in(seeds[1], 1), 0, 1),
        "aggregated": gaussian(seeds[2], (NODES, FIN), NODES ** -0.5, 0.03125, ((0, 128), (1, 8))),
        "weight": gaussian(seeds[3], (FIN, FOUT), FOUT ** -0.5, 0.1875, ((0, 8),)),
        "adj_tiles": gaussian(seeds[4], (N_ROW, N_COL, TILES_DEV, TILE, TILE), (TILE * TILES_DEV * TILE // (2 * NODES_DEV)) ** -0.5, 0.078125, ((0, 8), (1, 16))),
        "tile_row": with_ends(jax.random.randint(seeds[5], (N_ROW, N_COL, TILES_DEV), 0, NODES_DEV * N_COL // TILE), jax.random.fold_in(seeds[5], 1), 0, (NODES_DEV * N_COL // TILE) - 1).astype(jnp.int32),
        "tile_col": with_ends(jax.random.randint(seeds[6], (N_ROW, N_COL, TILES_DEV), 0, NODES_DEV * N_ROW // TILE), jax.random.fold_in(seeds[6], 1), 0, (NODES_DEV * N_ROW // TILE) - 1).astype(jnp.int32),
        "tile_count": draw_tile_count(jax.random.fold_in(seeds[8], 71), 0),
    }


def reference(grad_out, relu_mask, aggregated, weight, adj_tiles, tile_row, tile_col, tile_count):
    masked = grad_out * relu_mask.astype(jnp.bfloat16)
    back = jnp.dot(masked, weight.T, preferred_element_type=jnp.float32).astype(jnp.bfloat16)
    grad_weight = jnp.dot(aggregated.T, masked, preferred_element_type=jnp.float32)
    total_nodes = grad_out.shape[0]
    block_rows = total_nodes // N_ROW
    block_cols = total_nodes // N_COL
    tile_rows = block_rows // TILE
    width = back.shape[1]

    def one_block(running, device):
        row_block = (device // N_COL).astype(jnp.int32)
        col_block = (device % N_COL).astype(jnp.int32)
        panel = lax.dynamic_slice_in_dim(back, (col_block * block_cols).astype(jnp.int32), block_cols, 0)
        tile_data = adj_tiles[row_block, col_block].astype(jnp.float32)
        row_ids = tile_row[row_block, col_block]
        col_ids = tile_col[row_block, col_block]
        live_count = tile_count[row_block, col_block]
        gathered = panel.reshape(block_cols // TILE, TILE, width)[col_ids].astype(jnp.float32)
        products = jnp.einsum('tij,tjf->tif', tile_data, gathered, precision=lax.Precision.HIGHEST)
        is_live = jnp.arange(TILES_DEV, dtype=jnp.int32) < live_count
        picker = ((row_ids[None, :] == jnp.arange(tile_rows, dtype=jnp.int32)[:, None]) & is_live[None, :]).astype(jnp.float32)
        partial_value = jnp.einsum('kt,tif->kif', picker, products, precision=lax.Precision.HIGHEST).reshape(block_rows, width)
        rounded = lax.optimization_barrier(partial_value.astype(jnp.bfloat16))
        partial_value = rounded.astype(jnp.float32)
        offset = (row_block * block_rows).astype(jnp.int32)
        current = lax.dynamic_slice_in_dim(running, offset, block_rows, 0)
        running = lax.dynamic_update_slice_in_dim(running, current + partial_value, offset, 0)
        return running, None

    start_sum = jnp.zeros((total_nodes, width), jnp.float32)
    summed, _ = lax.scan(one_block, start_sum, jnp.arange(N_ROW * N_COL, dtype=jnp.int32))
    return summed.astype(jnp.bfloat16), grad_weight
```

```python
import jax
import jax.numpy as jnp
from jax import lax
from jax.experimental import pallas as pl
from jax.experimental.pallas import tpu as pltpu
from jax.sharding import PartitionSpec as P

LANES = 128
GROUP = 8
CHUNK = 16
VMEM = pl.BlockSpec(memory_space=pltpu.VMEM)
SMEM = pl.BlockSpec(memory_space=pltpu.SMEM)
HBM = pl.BlockSpec(memory_space=pl.ANY)


def params(mib):
    return pltpu.CompilerParams(vmem_limit_bytes=mib * 2**20)


def cost(flops, moved):
    return pl.CostEstimate(flops=flops, bytes_accessed=moved, transcendentals=0)


def panel_kernel(grad_ref, mask_ref, weight_ref, panel_ref, masked_ref):
    masked = grad_ref[...] * mask_ref[...].astype(jnp.float32).astype(jnp.bfloat16)
    masked_ref[...] = masked
    panel_ref[...] = lax.dot_general(
        masked, weight_ref[...], (((1,), (1,)), ((), ())), preferred_element_type=jnp.float32
    ).astype(jnp.bfloat16)


def weight_kernel(aggregated_ref, masked_ref, out_ref):
    flipped = aggregated_ref[...].T
    feats = flipped.shape[0]
    for j in range(masked_ref.shape[1] // LANES):
        term = jnp.dot(
            flipped, masked_ref[:, j * LANES : (j + 1) * LANES], preferred_element_type=jnp.float32
        )
        out_ref[j * feats : (j + 1) * feats, :] = term.astype(jnp.bfloat16)


def tiles_kernel(
    live_ref, row_ref, col_ref, tiles_hbm, near, four, two, one, weight_term, out_ref,
    tiles, panel, total, arrived,
):
    slots, size = tiles.shape[0], tiles.shape[1]
    copies = []
    for k in range(slots // CHUNK):
        part = pl.ds(k * CHUNK, CHUNK)
        copies.append(pltpu.make_async_copy(tiles_hbm.at[part], tiles.at[part], arrived.at[k]))
        copies[-1].start()
    total[...] = jnp.zeros_like(total)
    place = 0
    for part in (near, four, two, one):
        for k in range(part.shape[0] // size):
            panel[place] = part[k * size : (k + 1) * size, :]
            place += 1
    live = live_ref[0]

    def group(g, carry):
        first = g * GROUP
        terms = []
        for u in range(GROUP):
            terms.append(
                jnp.dot(
                    tiles[first + u], panel[col_ref[first + u]], preferred_element_type=jnp.float32
                )
            )
        for u in range(GROUP):
            r = row_ref[first + u]
            total[r] = total[r] + terms[u]
        return carry

    for k in range(slots // CHUNK):
        copies[k].wait()
        last = jnp.minimum((k + 1) * CHUNK, live)
        lax.fori_loop(k * CHUNK // GROUP, (last + GROUP - 1) // GROUP, group, 0)
    owners, height = out_ref.shape[0], out_ref.shape[1]
    extra = weight_term.shape[0]
    own = height - extra
    for c in range(owners):
        for k in range(own // size):
            out_ref[c, k * size : (k + 1) * size, :] = total[c * (own // size) + k].astype(
                jnp.bfloat16
            )
        out_ref[c, own:, :] = weight_term[...]


def finish_kernel(got_ref, features_ref, weight_ref):
    owners, height = got_ref.shape[0], got_ref.shape[1]
    own, feats = features_ref.shape[0], weight_ref.shape[0]
    extra = height - own
    for k in range(own // feats):
        rows = slice(k * feats, (k + 1) * feats)
        acc = got_ref[0, rows, :].astype(jnp.float32)
        for c in range(1, owners):
            acc = acc + got_ref[c, rows, :].astype(jnp.float32)
        features_ref[rows, :] = acc.astype(jnp.bfloat16)
    step = min(extra, feats)
    for g in range(0, owners * extra, step):
        c, at = g // extra, g % extra
        j, f = g // feats, g % feats
        weight_ref[f : f + step, j * LANES : (j + 1) * LANES] = got_ref[
            c, own + at : own + at + step, :
        ].astype(jnp.float32)


def shards(grad_out, relu_mask, aggregated, weight, adj_tiles, tile_row, tile_col, tile_count):
    n_row, n_col = lax.axis_size("row"), lax.axis_size("col")
    nodes, width = grad_out.shape
    feats = weight.shape[0]
    tile_data = adj_tiles[0, 0]
    slots, size = tile_data.shape[0], tile_data.shape[1]
    block_tiles = nodes * n_col // size
    per_owner = nodes // size
    bf, f32 = jnp.bfloat16, jnp.float32

    def swap(value, mask):
        return lax.ppermute(value, "row", [(i, i ^ mask) for i in range(n_row)])

    near, masked = pl.pallas_call(
        panel_kernel,
        out_shape=(
            jax.ShapeDtypeStruct((nodes, feats), bf),
            jax.ShapeDtypeStruct((nodes, width), bf),
        ),
        in_specs=[VMEM] * 3,
        out_specs=(VMEM, VMEM),
        compiler_params=params(16),
        cost_estimate=cost(2 * nodes * width * feats, nodes * width * 8),
    )(grad_out, relu_mask, weight)

    four = swap(near, 4)

    term = pl.pallas_call(
        weight_kernel,
        out_shape=jax.ShapeDtypeStruct((width // LANES * feats, LANES), bf),
        in_specs=[VMEM] * 2,
        out_specs=VMEM,
        compiler_params=params(16),
        cost_estimate=cost(2 * nodes * width * feats, nodes * width * 4),
    )(aggregated, masked)
    extra = term.shape[0] // n_col
    spread = lax.all_to_all(term.reshape(n_col, extra, LANES), "col", 0, 0, tiled=True)
    share = jnp.sum(spread.astype(f32), axis=0)

    two = swap(jnp.concatenate([near, four]), 2)
    share = share + swap(share, 4)
    one = swap(jnp.concatenate([near, four, two]), 1)
    share = share + swap(share, 2)
    share = share + swap(share, 1)

    live = tile_count[0, 0]
    away = (tile_col[0, 0] * size // nodes) ^ lax.axis_index("row")
    chunk = (away & 1) * 4 + (away & 2) + (away >> 2)
    col_at = chunk * per_owner + tile_col[0, 0] % per_owner
    row_at = jnp.where(jnp.arange(slots, dtype=jnp.int32) < live, tile_row[0, 0], block_tiles)

    sent = pl.pallas_call(
        tiles_kernel,
        out_shape=jax.ShapeDtypeStruct((n_col, nodes + extra, feats), bf),
        in_specs=[SMEM] * 3 + [HBM] + [VMEM] * 5,
        out_specs=VMEM,
        scratch_shapes=[
            pltpu.VMEM((slots, size, size), bf),
            pltpu.VMEM((n_row * per_owner, size, feats), bf),
            pltpu.VMEM((block_tiles + 1, size, feats), f32),
            pltpu.SemaphoreType.DMA((slots // CHUNK,)),
        ],
        compiler_params=params(32),
        cost_estimate=cost(2 * slots * size * size * feats, slots * size * size * 2),
    )(live.reshape(1), row_at, col_at, tile_data, near, four, two, one, share.astype(bf))
    got = lax.all_to_all(sent, "col", 0, 0, tiled=True)
    return pl.pallas_call(
        finish_kernel,
        out_shape=(
            jax.ShapeDtypeStruct((nodes, feats), bf),
            jax.ShapeDtypeStruct((feats, width), f32),
        ),
        in_specs=[VMEM],
        out_specs=(VMEM, VMEM),
        compiler_params=params(16),
        cost_estimate=cost(nodes * feats * n_col, nodes * feats * n_col * 2),
    )(got)


def solution(mesh):
    placed = (
        P(("col", "row"), None),
        P(("col", "row"), None),
        P(("col", "row"), "depth"),
        P("depth", None),
        P("row", "col", None, None, None),
        P("row", "col", None),
        P("row", "col", None),
        P("row", "col"),
    )
    return jax.shard_map(
        shards,
        mesh=mesh,
        in_specs=placed,
        out_specs=(P(("row", "col"), "depth"), P("depth", None)),
        check_vma=False,
    )
```

```python
import jax
import jax.numpy as jnp
from jax import lax
from jax.experimental import pallas as pl
from jax.experimental.pallas import tpu as pltpu
from jax.sharding import PartitionSpec as P

LANES = 128
GROUP = 8
PAIR = 2
VMEM = pl.BlockSpec(memory_space=pltpu.VMEM)
SMEM = pl.BlockSpec(memory_space=pltpu.SMEM)
HBM = pl.BlockSpec(memory_space=pl.ANY)


def params(mib):
    return pltpu.CompilerParams(vmem_limit_bytes=int(mib * 2**20))


def cost(flops, moved):
    return pl.CostEstimate(flops=flops, bytes_accessed=moved, transcendentals=0)


def panel_kernel(grad_hbm, mask_hbm, weight_hbm, panel_ref, grad, mask, weight, arrived):
    copies = [
        pltpu.make_async_copy(mask_hbm, mask, arrived.at[0]),
        pltpu.make_async_copy(grad_hbm, grad, arrived.at[1]),
        pltpu.make_async_copy(weight_hbm, weight, arrived.at[2]),
    ]
    for copy in copies:
        copy.start()
    for copy in copies:
        copy.wait()
    masked = grad[...] * mask[...].astype(jnp.float32).astype(jnp.bfloat16)
    panel_ref[...] = lax.dot_general(
        masked, weight[...], (((1,), (1,)), ((), ())), preferred_element_type=jnp.float32
    ).astype(jnp.bfloat16)


def weight_kernel(
    grad_hbm, mask_hbm, aggregated_hbm, after_ref, out_ref, grad, mask, aggregated, arrived
):
    copies = [
        pltpu.make_async_copy(mask_hbm, mask, arrived.at[0]),
        pltpu.make_async_copy(grad_hbm, grad, arrived.at[1]),
        pltpu.make_async_copy(aggregated_hbm, aggregated, arrived.at[2]),
    ]
    for copy in copies:
        copy.start()
    for copy in copies:
        copy.wait()
    flipped = aggregated[...].T
    feats = flipped.shape[0]
    for j in range(grad.shape[1] // LANES):
        part = slice(j * LANES, (j + 1) * LANES)
        masked = grad[:, part] * mask[:, part].astype(jnp.float32).astype(jnp.bfloat16)
        term = jnp.dot(flipped, masked, preferred_element_type=jnp.float32)
        out_ref[j * feats : (j + 1) * feats, :] = term.astype(jnp.bfloat16)


def pack_kernel(spread_ref, near, four, packed_ref):
    acc = spread_ref[0].astype(jnp.float32)
    for c in range(1, spread_ref.shape[0]):
        acc = acc + spread_ref[c].astype(jnp.float32)
    nodes = near.shape[0]
    packed_ref[0:nodes, :] = near[...]
    packed_ref[nodes : 2 * nodes, :] = four[...]
    packed_ref[2 * nodes :, :] = acc.astype(jnp.bfloat16)


def tiles_kernel(
    live_ref, row_ref, col_ref, tiles, near, four, got_1, got_2, got_3, out_ref, panel, total
):
    size = tiles.shape[1]
    total[...] = jnp.zeros_like(total)
    per_owner = near.shape[0] // size
    place = 0
    for part, count in (
        (near, per_owner),
        (four, per_owner),
        (got_1, 2 * per_owner),
        (got_2, 2 * per_owner),
        (got_3, 2 * per_owner),
    ):
        for k in range(count):
            panel[place] = part[k * size : (k + 1) * size, :]
            place += 1

    def group(g, carry):
        first = g * GROUP
        terms = []
        for u in range(GROUP):
            terms.append(
                jnp.dot(
                    tiles[first + u], panel[col_ref[first + u]], preferred_element_type=jnp.float32
                )
            )
        for u in range(GROUP):
            r = row_ref[first + u]
            total[r] = total[r] + terms[u]
        return carry

    lax.fori_loop(0, (live_ref[0] + GROUP - 1) // GROUP, group, 0)
    owners, height = out_ref.shape[0], out_ref.shape[1]
    for c in range(owners):
        for k in range(height // size):
            out_ref[c, k * size : (k + 1) * size, :] = total[c * (height // size) + k].astype(
                jnp.bfloat16
            )


def halves_kernel(half_ref, got_ref, keep_ref, send_ref, total):
    owners, height = got_ref.shape[0], got_ref.shape[1]
    for k in range(height // LANES):
        rows = slice(k * LANES, (k + 1) * LANES)
        acc = got_ref[0, rows, :].astype(jnp.float32)
        for c in range(1, owners):
            acc = acc + got_ref[c, rows, :].astype(jnp.float32)
        total[rows, :] = acc
    own = keep_ref.shape[0]
    half = half_ref[0]
    keep_ref[...] = total[pl.ds(pl.multiple_of(half * own, own), own), :]
    send_ref[...] = total[pl.ds(pl.multiple_of((1 - half) * own, own), own), :].astype(jnp.bfloat16)


def share_kernel(after_ref, own, got_4, got_pair, got_both, out_ref):
    f32 = jnp.float32
    total = (own[...].astype(f32) + got_4[...].astype(f32)) + (
        got_pair[...].astype(f32) + got_both[...].astype(f32)
    )
    total = total.astype(jnp.bfloat16)
    for c in range(out_ref.shape[0]):
        out_ref[c] = total


def finish_kernel(keep_ref, got_ref, shares_ref, features_ref, weight_ref):
    features_ref[...] = (keep_ref[...] + got_ref[...].astype(jnp.float32)).astype(jnp.bfloat16)
    owners, rows = shares_ref.shape[0], shares_ref.shape[1]
    feats = weight_ref.shape[0]
    for g in range(owners * rows // feats):
        c, at = g * feats // rows, g * feats % rows
        weight_ref[:, g * LANES : (g + 1) * LANES] = shares_ref[c, at : at + feats, :].astype(
            jnp.float32
        )


def shards(grad_out, relu_mask, aggregated, weight, adj_tiles, tile_row, tile_col, tile_count):
    n_row, n_col = lax.axis_size("row"), lax.axis_size("col")
    n_y = n_col // PAIR
    lines = [[y * PAIR + h for y in range(n_y)] for h in range(PAIR)]
    nodes, width = grad_out.shape
    feats = weight.shape[0]
    tile_data = adj_tiles[0, 0]
    slots, size = tile_data.shape[0], tile_data.shape[1]
    block_tiles = nodes * n_col // size
    per_owner = nodes // size
    bf, f32 = jnp.bfloat16, jnp.float32
    shape = jax.ShapeDtypeStruct

    def swap(value, mask):
        return lax.ppermute(value, "row", [(i, i ^ mask) for i in range(n_row)])

    def swap_pair(value, mask=0):
        if mask == 0:
            return lax.ppermute(value, "col", [(i, i ^ 1) for i in range(n_col)])
        count = n_row * n_col
        return lax.ppermute(
            value, ("row", "col"), [(i, i ^ (mask * n_col + 1)) for i in range(count)]
        )

    def line_all_to_all(value):
        return lax.all_to_all(value, "col", 0, 0, axis_index_groups=lines, tiled=True)

    near = pl.pallas_call(
        panel_kernel,
        out_shape=shape((nodes, feats), bf),
        in_specs=[HBM] * 3,
        out_specs=VMEM,
        scratch_shapes=[
            pltpu.VMEM((nodes, width), bf),
            pltpu.VMEM((nodes, width), jnp.int32),
            pltpu.VMEM((feats, width), bf),
            pltpu.SemaphoreType.DMA((3,)),
        ],
        compiler_params=params(53.75),
        cost_estimate=cost(2 * nodes * width * feats, nodes * width * 8),
    )(grad_out, relu_mask, weight)

    four = swap(near, 4)

    term = pl.pallas_call(
        weight_kernel,
        out_shape=shape((width // LANES * feats, LANES), bf),
        in_specs=[HBM] * 4,
        out_specs=VMEM,
        scratch_shapes=[
            pltpu.VMEM((nodes, width), bf),
            pltpu.VMEM((nodes, width), jnp.int32),
            pltpu.VMEM((nodes, feats), bf),
            pltpu.SemaphoreType.DMA((3,)),
        ],
        compiler_params=params(53),
        cost_estimate=cost(2 * 10**10, nodes * width * 4),
    )(grad_out, relu_mask, aggregated, near)
    spread = line_all_to_all(term.reshape(n_y, term.shape[0] // n_y, LANES))
    extra = spread.shape[1]
    packed = pl.pallas_call(
        pack_kernel,
        out_shape=shape((2 * nodes + extra, LANES), bf),
        in_specs=[VMEM] * 3,
        out_specs=VMEM,
        compiler_params=params(16),
        cost_estimate=cost(nodes * feats * n_y, nodes * feats * n_y * 2),
    )(spread, near, four)
    got_1, got_2, got_3 = swap(packed, 1), swap(packed, 2), swap(packed, 3)

    def tail(value):
        return value[2 * nodes :].astype(f32)

    share = ((tail(packed) + tail(got_1)) + (tail(got_2) + tail(got_3))).astype(bf)
    far_4, far_pair, far_both = swap(share, 4), swap_pair(share), swap_pair(share, 4)

    live = tile_count[0, 0]
    away = (tile_col[0, 0] * size // nodes) ^ lax.axis_index("row")
    chunk = (away & 3) * 2 + (away >> 2)
    col_at = chunk * per_owner + tile_col[0, 0] % per_owner
    row_at = jnp.where(jnp.arange(slots, dtype=jnp.int32) < live, tile_row[0, 0], block_tiles)

    sent = pl.pallas_call(
        tiles_kernel,
        out_shape=shape((n_y, PAIR * nodes, feats), bf),
        in_specs=[SMEM] * 3 + [VMEM] * 6,
        out_specs=VMEM,
        scratch_shapes=[
            pltpu.VMEM((n_row * per_owner, size, feats), bf),
            pltpu.VMEM((block_tiles + 1, size, feats), f32),
        ],
        compiler_params=params(32),
        cost_estimate=cost(2 * 10**10, slots * size * size * 2),
    )(live.reshape(1), row_at, col_at, tile_data, near, four, got_1, got_2, got_3)
    got = line_all_to_all(sent)
    half = (lax.axis_index("col") & (PAIR - 1)).astype(jnp.int32).reshape(1)
    keep, send = pl.pallas_call(
        halves_kernel,
        out_shape=(shape((nodes, feats), f32), shape((nodes, feats), bf)),
        in_specs=[SMEM, VMEM],
        out_specs=(VMEM, VMEM),
        scratch_shapes=[pltpu.VMEM((PAIR * nodes, feats), f32)],
        compiler_params=params(16),
        cost_estimate=cost(nodes * feats * n_col, nodes * feats * n_col * 2),
    )(half, got)
    other = swap_pair(send)
    whole = pl.pallas_call(
        share_kernel,
        out_shape=shape((n_y, extra, LANES), bf),
        in_specs=[HBM] + [VMEM] * 4,
        out_specs=VMEM,
        compiler_params=params(16),
        cost_estimate=cost(2 * 10**10, n_y * extra * LANES * 2),
    )(send, share, far_4, far_pair, far_both)
    shares = line_all_to_all(whole)
    return pl.pallas_call(
        finish_kernel,
        out_shape=(shape((nodes, feats), bf), shape((feats, width), f32)),
        in_specs=[VMEM] * 3,
        out_specs=(VMEM, VMEM),
        compiler_params=params(16),
        cost_estimate=cost(nodes * feats, feats * width * 6),
    )(keep, other, shares)


def solution(mesh):
    placed = (
        P(("col", "row"), None),
        P(("col", "row"), None),
        P(("col", "row"), "depth"),
        P("depth", None),
        P("row", "col", None, None, None),
        P("row", "col", None),
        P("row", "col", None),
        P("row", "col"),
    )
    return jax.shard_map(
        shards,
        mesh=mesh,
        in_specs=placed,
        out_specs=(P(("row", "col"), "depth"), P("depth", None)),
        check_vma=False,
    )
```

```python
import jax
import jax.numpy as jnp
from jax import lax
from jax.experimental import pallas as pl
from jax.experimental.pallas import tpu as pltpu
from jax.sharding import PartitionSpec as P

LANES = 128
GROUP = 8
CHUNK = 16
PAIR = 2
VMEM = pl.BlockSpec(memory_space=pltpu.VMEM)
SMEM = pl.BlockSpec(memory_space=pltpu.SMEM)
HBM = pl.BlockSpec(memory_space=pl.ANY)


def params(mib):
    return pltpu.CompilerParams(vmem_limit_bytes=int(mib * 2**20))


def cost(flops, moved):
    return pl.CostEstimate(flops=flops, bytes_accessed=moved, transcendentals=0)


def panel_kernel(grad_hbm, mask_hbm, weight_hbm, panel_ref, grad, mask, weight, arrived):
    copies = [
        pltpu.make_async_copy(mask_hbm, mask, arrived.at[0]),
        pltpu.make_async_copy(grad_hbm, grad, arrived.at[1]),
        pltpu.make_async_copy(weight_hbm, weight, arrived.at[2]),
    ]
    for copy in copies:
        copy.start()
    for copy in copies:
        copy.wait()
    masked = grad[...] * mask[...].astype(jnp.float32).astype(jnp.bfloat16)
    panel_ref[...] = lax.dot_general(
        masked, weight[...], (((1,), (1,)), ((), ())), preferred_element_type=jnp.float32
    ).astype(jnp.bfloat16)


def weight_kernel(
    grad_hbm, mask_hbm, aggregated_hbm, after_ref, out_ref, grad, mask, aggregated, arrived
):
    copies = [
        pltpu.make_async_copy(mask_hbm, mask, arrived.at[0]),
        pltpu.make_async_copy(grad_hbm, grad, arrived.at[1]),
        pltpu.make_async_copy(aggregated_hbm, aggregated, arrived.at[2]),
    ]
    for copy in copies:
        copy.start()
    for copy in copies:
        copy.wait()
    flipped = aggregated[...].T
    feats = flipped.shape[0]
    for j in range(grad.shape[1] // LANES):
        part = slice(j * LANES, (j + 1) * LANES)
        masked = grad[:, part] * mask[:, part].astype(jnp.float32).astype(jnp.bfloat16)
        term = jnp.dot(flipped, masked, preferred_element_type=jnp.float32)
        out_ref[j * feats : (j + 1) * feats, :] = term.astype(jnp.bfloat16)


def sum_kernel(after_ref, spread_ref, out_ref):
    acc = spread_ref[0].astype(jnp.float32)
    for c in range(1, spread_ref.shape[0]):
        acc = acc + spread_ref[c].astype(jnp.float32)
    out_ref[...] = acc.astype(jnp.bfloat16)


def tiles_kernel(
    live_ref, row_ref, col_ref, tiles_hbm, near, four, got_1, got_2, got_3, out_ref,
    tiles, panel, total, arrived,
):
    slots, size = tiles.shape[0], tiles.shape[1]
    copies = []
    for k in range(slots // CHUNK):
        part = pl.ds(k * CHUNK, CHUNK)
        copies.append(pltpu.make_async_copy(tiles_hbm.at[part], tiles.at[part], arrived.at[k]))
        copies[-1].start()
    total[...] = jnp.zeros_like(total)
    place = 0
    for part in (near, four, got_1, got_2, got_3):
        for k in range(part.shape[0] // size):
            panel[place] = part[k * size : (k + 1) * size, :]
            place += 1
    live = live_ref[0]

    def group(g, carry):
        first = g * GROUP
        terms = []
        for u in range(GROUP):
            terms.append(
                jnp.dot(
                    tiles[first + u], panel[col_ref[first + u]], preferred_element_type=jnp.float32
                )
            )
        for u in range(GROUP):
            r = row_ref[first + u]
            total[r] = total[r] + terms[u]
        return carry

    for k in range(slots // CHUNK):
        copies[k].wait()
        last = jnp.minimum((k + 1) * CHUNK, live)
        lax.fori_loop(k * CHUNK // GROUP, (last + GROUP - 1) // GROUP, group, 0)
    owners, height = out_ref.shape[0], out_ref.shape[1]
    for c in range(owners):
        for k in range(height // size):
            out_ref[c, k * size : (k + 1) * size, :] = total[c * (height // size) + k].astype(
                jnp.bfloat16
            )


def halves_kernel(half_ref, got_ref, keep_ref, send_ref, total):
    owners, height = got_ref.shape[0], got_ref.shape[1]
    for k in range(height // LANES):
        rows = slice(k * LANES, (k + 1) * LANES)
        acc = got_ref[0, rows, :].astype(jnp.float32)
        for c in range(1, owners):
            acc = acc + got_ref[c, rows, :].astype(jnp.float32)
        total[rows, :] = acc
    own = keep_ref.shape[0]
    half = half_ref[0]
    keep_ref[...] = total[pl.ds(pl.multiple_of(half * own, own), own), :]
    send_ref[...] = total[pl.ds(pl.multiple_of((1 - half) * own, own), own), :].astype(jnp.bfloat16)


def share_kernel(after_ref, own, got_4, got_pair, got_both, out_ref):
    f32 = jnp.float32
    total = (own[...].astype(f32) + got_4[...].astype(f32)) + (
        got_pair[...].astype(f32) + got_both[...].astype(f32)
    )
    total = total.astype(jnp.bfloat16)
    for c in range(out_ref.shape[0]):
        out_ref[c] = total


def features_kernel(keep_ref, got_ref, features_ref, after_ref):
    after_ref[...] = jnp.zeros_like(after_ref)
    features_ref[...] = (keep_ref[...] + got_ref[...].astype(jnp.float32)).astype(jnp.bfloat16)


def spread_kernel(after_ref, shares_ref, weight_ref):
    owners, rows = shares_ref.shape[0], shares_ref.shape[1]
    feats = weight_ref.shape[0]
    for g in range(owners * rows // feats):
        c, at = g * feats // rows, g * feats % rows
        weight_ref[:, g * LANES : (g + 1) * LANES] = shares_ref[c, at : at + feats, :].astype(
            jnp.float32
        )


def shards(grad_out, relu_mask, aggregated, weight, adj_tiles, tile_row, tile_col, tile_count):
    n_row, n_col = lax.axis_size("row"), lax.axis_size("col")
    n_y = n_col // PAIR
    lines = [[y * PAIR + h for y in range(n_y)] for h in range(PAIR)]
    nodes, width = grad_out.shape
    feats = weight.shape[0]
    tile_data = adj_tiles[0, 0]
    slots, size = tile_data.shape[0], tile_data.shape[1]
    block_tiles = nodes * n_col // size
    per_owner = nodes // size
    bf, f32 = jnp.bfloat16, jnp.float32
    shape = jax.ShapeDtypeStruct

    def swap(value, mask):
        return lax.ppermute(value, "row", [(i, i ^ mask) for i in range(n_row)])

    def swap_pair(value, mask=0):
        if mask == 0:
            return lax.ppermute(value, "col", [(i, i ^ 1) for i in range(n_col)])
        count = n_row * n_col
        return lax.ppermute(
            value, ("row", "col"), [(i, i ^ (mask * n_col + 1)) for i in range(count)]
        )

    def line_all_to_all(value):
        return lax.all_to_all(value, "col", 0, 0, axis_index_groups=lines, tiled=True)

    near = pl.pallas_call(
        panel_kernel,
        out_shape=shape((nodes, feats), bf),
        in_specs=[HBM] * 3,
        out_specs=VMEM,
        scratch_shapes=[
            pltpu.VMEM((nodes, width), bf),
            pltpu.VMEM((nodes, width), jnp.int32),
            pltpu.VMEM((feats, width), bf),
            pltpu.SemaphoreType.DMA((3,)),
        ],
        compiler_params=params(53.75),
        cost_estimate=cost(2 * nodes * width * feats, nodes * width * 8),
    )(grad_out, relu_mask, weight)

    four = swap(near, 4)

    term = pl.pallas_call(
        weight_kernel,
        out_shape=shape((width // LANES * feats, LANES), bf),
        in_specs=[HBM] * 4,
        out_specs=VMEM,
        scratch_shapes=[
            pltpu.VMEM((nodes, width), bf),
            pltpu.VMEM((nodes, width), jnp.int32),
            pltpu.VMEM((nodes, feats), bf),
            pltpu.SemaphoreType.DMA((3,)),
        ],
        compiler_params=params(54),
        cost_estimate=cost(2 * 10**10, nodes * width * 4),
    )(grad_out, relu_mask, aggregated, four)
    spread = line_all_to_all(term.reshape(n_y, term.shape[0] // n_y, LANES))
    extra = spread.shape[1]
    packed = jnp.concatenate([near, four])
    got_1, got_2, got_3 = swap(packed, 1), swap(packed, 2), swap(packed, 3)

    live = tile_count[0, 0]
    away = (tile_col[0, 0] * size // nodes) ^ lax.axis_index("row")
    chunk = (away & 3) * 2 + (away >> 2)
    col_at = chunk * per_owner + tile_col[0, 0] % per_owner
    row_at = jnp.where(jnp.arange(slots, dtype=jnp.int32) < live, tile_row[0, 0], block_tiles)

    sent = pl.pallas_call(
        tiles_kernel,
        out_shape=shape((n_y, PAIR * nodes, feats), bf),
        in_specs=[SMEM] * 3 + [HBM] + [VMEM] * 5,
        out_specs=VMEM,
        scratch_shapes=[
            pltpu.VMEM((slots, size, size), bf),
            pltpu.VMEM((n_row * per_owner, size, feats), bf),
            pltpu.VMEM((block_tiles + 1, size, feats), f32),
            pltpu.SemaphoreType.DMA((slots // CHUNK,)),
        ],
        compiler_params=params(50),
        cost_estimate=cost(2 * 10**10, slots * size * size * 2),
    )(live.reshape(1), row_at, col_at, tile_data, near, four, got_1, got_2, got_3)
    got = line_all_to_all(sent)

    share = pl.pallas_call(
        sum_kernel,
        out_shape=shape((extra, LANES), bf),
        in_specs=[HBM, VMEM],
        out_specs=VMEM,
        compiler_params=params(16),
        cost_estimate=cost(n_y * extra * LANES, n_y * extra * LANES * 2),
    )(sent, spread)
    row_1, row_2, row_3 = swap(share, 1), swap(share, 2), swap(share, 3)
    share = ((share.astype(f32) + row_1.astype(f32)) + (row_2.astype(f32) + row_3.astype(f32))).astype(bf)
    far_4, far_pair, far_both = swap(share, 4), swap_pair(share), swap_pair(share, 4)

    half = (lax.axis_index("col") & (PAIR - 1)).astype(jnp.int32).reshape(1)
    keep, send = pl.pallas_call(
        halves_kernel,
        out_shape=(shape((nodes, feats), f32), shape((nodes, feats), bf)),
        in_specs=[SMEM, VMEM],
        out_specs=(VMEM, VMEM),
        scratch_shapes=[pltpu.VMEM((PAIR * nodes, feats), f32)],
        compiler_params=params(16),
        cost_estimate=cost(nodes * feats * n_col, nodes * feats * n_col * 2),
    )(half, got)
    other = swap_pair(send)
    whole = pl.pallas_call(
        share_kernel,
        out_shape=shape((n_y, extra, LANES), bf),
        in_specs=[HBM] + [VMEM] * 4,
        out_specs=VMEM,
        compiler_params=params(16),
        cost_estimate=cost(2 * 10**10, n_y * extra * LANES * 2),
    )(send, share, far_4, far_pair, far_both)
    shares = line_all_to_all(whole)
    features, after = pl.pallas_call(
        features_kernel,
        out_shape=(shape((nodes, feats), bf), shape((8, LANES), f32)),
        in_specs=[VMEM] * 2,
        out_specs=(VMEM, VMEM),
        compiler_params=params(16),
        cost_estimate=cost(2 * 10**10, nodes * feats * 4),
    )(keep, other)
    grad_weight = pl.pallas_call(
        spread_kernel,
        out_shape=shape((feats, width), f32),
        in_specs=[HBM, VMEM],
        out_specs=VMEM,
        compiler_params=params(16),
        cost_estimate=cost(feats * width, feats * width * 6),
    )(after, shares)
    return features, grad_weight


def solution(mesh):
    placed = (
        P(("col", "row"), None),
        P(("col", "row"), None),
        P(("col", "row"), "depth"),
        P("depth", None),
        P("row", "col", None, None, None),
        P("row", "col", None),
        P("row", "col", None),
        P("row", "col"),
    )
    return jax.shard_map(
        shards,
        mesh=mesh,
        in_specs=placed,
        out_specs=(P(("row", "col"), "depth"), P("depth", None)),
        check_vma=False,
    )
```

```python
import jax
import jax.numpy as jnp
from jax import lax
from jax.experimental import pallas as pl
from jax.experimental.pallas import tpu as pltpu
from jax.sharding import PartitionSpec as P

LANES = 128
GROUP = 8
CHUNK = 16
PAIR = 2
VMEM = pl.BlockSpec(memory_space=pltpu.VMEM)
SMEM = pl.BlockSpec(memory_space=pltpu.SMEM)
HBM = pl.BlockSpec(memory_space=pl.ANY)


def params(mib):
    return pltpu.CompilerParams(vmem_limit_bytes=int(mib * 2**20))


def cost(flops, moved):
    return pl.CostEstimate(flops=flops, bytes_accessed=moved, transcendentals=0)


def panel_kernel(grad_hbm, mask_hbm, weight_hbm, panel_ref, grad, mask, weight, arrived):
    copies = [
        pltpu.make_async_copy(mask_hbm, mask, arrived.at[0]),
        pltpu.make_async_copy(grad_hbm, grad, arrived.at[1]),
        pltpu.make_async_copy(weight_hbm, weight, arrived.at[2]),
    ]
    for copy in copies:
        copy.start()
    for copy in copies:
        copy.wait()
    masked = grad[...] * mask[...].astype(jnp.float32).astype(jnp.bfloat16)
    panel_ref[...] = lax.dot_general(
        masked, weight[...], (((1,), (1,)), ((), ())), preferred_element_type=jnp.float32
    ).astype(jnp.bfloat16)


def weight_kernel(
    grad_hbm, mask_hbm, aggregated_hbm, out_ref, grad, mask, aggregated, arrived
):
    copies = [
        pltpu.make_async_copy(mask_hbm, mask, arrived.at[0]),
        pltpu.make_async_copy(grad_hbm, grad, arrived.at[1]),
        pltpu.make_async_copy(aggregated_hbm, aggregated, arrived.at[2]),
    ]
    for copy in copies:
        copy.start()
    for copy in copies:
        copy.wait()
    flipped = aggregated[...].T
    feats = flipped.shape[0]
    for j in range(grad.shape[1] // LANES):
        part = slice(j * LANES, (j + 1) * LANES)
        masked = grad[:, part] * mask[:, part].astype(jnp.float32).astype(jnp.bfloat16)
        term = jnp.dot(flipped, masked, preferred_element_type=jnp.float32)
        out_ref[j * feats : (j + 1) * feats, :] = term.astype(jnp.bfloat16)


def token_kernel(four_ref, token_ref):
    token_ref[...] = jnp.zeros_like(token_ref)


def pack_kernel(token_ref, spread_ref, near, four, packed_ref):
    acc = spread_ref[0].astype(jnp.float32)
    for c in range(1, spread_ref.shape[0]):
        acc = acc + spread_ref[c].astype(jnp.float32)
    nodes = near.shape[0]
    packed_ref[0:nodes, :] = near[...]
    packed_ref[nodes : 2 * nodes, :] = four[...]
    packed_ref[2 * nodes :, :] = acc.astype(jnp.bfloat16)


def tiles_kernel(
    live_ref, row_ref, col_ref, tiles_hbm, near, four, got_1, got_2, got_3, out_ref,
    tiles, panel, total, arrived,
):
    slots, size = tiles.shape[0], tiles.shape[1]
    copies = []
    for k in range(slots // CHUNK):
        part = pl.ds(k * CHUNK, CHUNK)
        copies.append(pltpu.make_async_copy(tiles_hbm.at[part], tiles.at[part], arrived.at[k]))
        copies[-1].start()
    total[...] = jnp.zeros_like(total)
    place = 0
    for part in (near, four, got_1, got_2, got_3):
        for k in range(min(part.shape[0], 2 * near.shape[0]) // size):
            panel[place] = part[k * size : (k + 1) * size, :]
            place += 1
    live = live_ref[0]

    def group(g, carry):
        first = g * GROUP
        terms = []
        for u in range(GROUP):
            terms.append(
                jnp.dot(
                    tiles[first + u], panel[col_ref[first + u]], preferred_element_type=jnp.float32
                )
            )
        for u in range(GROUP):
            r = row_ref[first + u]
            total[r] = total[r] + terms[u]
        return carry

    for k in range(slots // CHUNK):
        copies[k].wait()
        last = jnp.minimum((k + 1) * CHUNK, live)
        lax.fori_loop(k * CHUNK // GROUP, (last + GROUP - 1) // GROUP, group, 0)
    owners, height = out_ref.shape[0], out_ref.shape[1]
    for c in range(owners):
        for k in range(height // size):
            out_ref[c, k * size : (k + 1) * size, :] = total[c * (height // size) + k].astype(
                jnp.bfloat16
            )


def halves_kernel(half_ref, got_ref, keep_ref, send_ref, total):
    owners, height = got_ref.shape[0], got_ref.shape[1]
    for k in range(height // LANES):
        rows = slice(k * LANES, (k + 1) * LANES)
        acc = got_ref[0, rows, :].astype(jnp.float32)
        for c in range(1, owners):
            acc = acc + got_ref[c, rows, :].astype(jnp.float32)
        total[rows, :] = acc
    own = keep_ref.shape[0]
    half = half_ref[0]
    keep_ref[...] = total[pl.ds(pl.multiple_of(half * own, own), own), :]
    send_ref[...] = total[pl.ds(pl.multiple_of((1 - half) * own, own), own), :].astype(jnp.bfloat16)


def share_kernel(after_ref, own, got_4, got_pair, got_both, out_ref):
    f32 = jnp.float32
    total = (own[...].astype(f32) + got_4[...].astype(f32)) + (
        got_pair[...].astype(f32) + got_both[...].astype(f32)
    )
    total = total.astype(jnp.bfloat16)
    for c in range(out_ref.shape[0]):
        out_ref[c] = total


def features_kernel(keep_ref, got_ref, features_ref, after_ref):
    after_ref[...] = jnp.zeros_like(after_ref)
    features_ref[...] = (keep_ref[...] + got_ref[...].astype(jnp.float32)).astype(jnp.bfloat16)


def spread_kernel(after_ref, shares_ref, weight_ref):
    owners, rows = shares_ref.shape[0], shares_ref.shape[1]
    feats = weight_ref.shape[0]
    for g in range(owners * rows // feats):
        c, at = g * feats // rows, g * feats % rows
        weight_ref[:, g * LANES : (g + 1) * LANES] = shares_ref[c, at : at + feats, :].astype(
            jnp.float32
        )


def shards(grad_out, relu_mask, aggregated, weight, adj_tiles, tile_row, tile_col, tile_count):
    n_row, n_col = lax.axis_size("row"), lax.axis_size("col")
    n_y = n_col // PAIR
    lines = [[y * PAIR + h for y in range(n_y)] for h in range(PAIR)]
    nodes, width = grad_out.shape
    feats = weight.shape[0]
    tile_data = adj_tiles[0, 0]
    slots, size = tile_data.shape[0], tile_data.shape[1]
    block_tiles = nodes * n_col // size
    per_owner = nodes // size
    bf, f32 = jnp.bfloat16, jnp.float32
    shape = jax.ShapeDtypeStruct

    def swap(value, mask):
        return lax.ppermute(value, "row", [(i, i ^ mask) for i in range(n_row)])

    def swap_pair(value, mask=0):
        if mask == 0:
            return lax.ppermute(value, "col", [(i, i ^ 1) for i in range(n_col)])
        count = n_row * n_col
        return lax.ppermute(
            value, ("row", "col"), [(i, i ^ (mask * n_col + 1)) for i in range(count)]
        )

    def line_all_to_all(value):
        return lax.all_to_all(value, "col", 0, 0, axis_index_groups=lines, tiled=True)

    near = pl.pallas_call(
        panel_kernel,
        out_shape=shape((nodes, feats), bf),
        in_specs=[HBM] * 3,
        out_specs=VMEM,
        scratch_shapes=[
            pltpu.VMEM((nodes, width), bf),
            pltpu.VMEM((nodes, width), jnp.int32),
            pltpu.VMEM((feats, width), bf),
            pltpu.SemaphoreType.DMA((3,)),
        ],
        compiler_params=params(53.75),
        cost_estimate=cost(2 * nodes * width * feats, nodes * width * 8),
    )(grad_out, relu_mask, weight)

    four = swap(near, 4)

    term = pl.pallas_call(
        weight_kernel,
        out_shape=shape((width // LANES * feats, LANES), bf),
        in_specs=[HBM] * 3,
        out_specs=VMEM,
        scratch_shapes=[
            pltpu.VMEM((nodes, width), bf),
            pltpu.VMEM((nodes, width), jnp.int32),
            pltpu.VMEM((nodes, feats), bf),
            pltpu.SemaphoreType.DMA((3,)),
        ],
        compiler_params=params(54),
        cost_estimate=cost(2 * 10**10, nodes * width * 4),
    )(grad_out, relu_mask, aggregated)
    spread = line_all_to_all(term.reshape(n_y, term.shape[0] // n_y, LANES))
    extra = spread.shape[1]
    token = pl.pallas_call(
        token_kernel,
        out_shape=shape((8, LANES), f32),
        in_specs=[HBM],
        out_specs=VMEM,
        compiler_params=params(16),
        cost_estimate=cost(2 * 10**10, 8 * LANES),
    )(four)
    packed = pl.pallas_call(
        pack_kernel,
        out_shape=shape((2 * nodes + extra, LANES), bf),
        in_specs=[HBM] + [VMEM] * 3,
        out_specs=VMEM,
        compiler_params=params(16),
        cost_estimate=cost(nodes * feats * n_y, nodes * feats * n_y * 2),
    )(token, spread, near, four)
    got_1, got_2, got_3 = swap(packed, 1), swap(packed, 2), swap(packed, 3)

    def tail(value):
        return value[2 * nodes :].astype(f32)

    live = tile_count[0, 0]
    away = (tile_col[0, 0] * size // nodes) ^ lax.axis_index("row")
    chunk = (away & 3) * 2 + (away >> 2)
    col_at = chunk * per_owner + tile_col[0, 0] % per_owner
    row_at = jnp.where(jnp.arange(slots, dtype=jnp.int32) < live, tile_row[0, 0], block_tiles)

    sent = pl.pallas_call(
        tiles_kernel,
        out_shape=shape((n_y, PAIR * nodes, feats), bf),
        in_specs=[SMEM] * 3 + [HBM] + [VMEM] * 5,
        out_specs=VMEM,
        scratch_shapes=[
            pltpu.VMEM((slots, size, size), bf),
            pltpu.VMEM((n_row * per_owner, size, feats), bf),
            pltpu.VMEM((block_tiles + 1, size, feats), f32),
            pltpu.SemaphoreType.DMA((slots // CHUNK,)),
        ],
        compiler_params=params(50),
        cost_estimate=cost(2 * 10**10, slots * size * size * 2),
    )(live.reshape(1), row_at, col_at, tile_data, near, four, got_1, got_2, got_3)
    got = line_all_to_all(sent)

    share = ((tail(packed) + tail(got_1)) + (tail(got_2) + tail(got_3))).astype(bf)
    far_4, far_pair, far_both = swap(share, 4), swap_pair(share), swap_pair(share, 4)

    half = (lax.axis_index("col") & (PAIR - 1)).astype(jnp.int32).reshape(1)
    keep, send = pl.pallas_call(
        halves_kernel,
        out_shape=(shape((nodes, feats), f32), shape((nodes, feats), bf)),
        in_specs=[SMEM, VMEM],
        out_specs=(VMEM, VMEM),
        scratch_shapes=[pltpu.VMEM((PAIR * nodes, feats), f32)],
        compiler_params=params(16),
        cost_estimate=cost(nodes * feats * n_col, nodes * feats * n_col * 2),
    )(half, got)
    other = swap_pair(send)
    whole = pl.pallas_call(
        share_kernel,
        out_shape=shape((n_y, extra, LANES), bf),
        in_specs=[HBM] + [VMEM] * 4,
        out_specs=VMEM,
        compiler_params=params(16),
        cost_estimate=cost(2 * 10**10, n_y * extra * LANES * 2),
    )(send, share, far_4, far_pair, far_both)
    shares = line_all_to_all(whole)
    features, after = pl.pallas_call(
        features_kernel,
        out_shape=(shape((nodes, feats), bf), shape((8, LANES), f32)),
        in_specs=[VMEM] * 2,
        out_specs=(VMEM, VMEM),
        compiler_params=params(16),
        cost_estimate=cost(2 * 10**10, nodes * feats * 4),
    )(keep, other)
    grad_weight = pl.pallas_call(
        spread_kernel,
        out_shape=shape((feats, width), f32),
        in_specs=[HBM, VMEM],
        out_specs=VMEM,
        compiler_params=params(16),
        cost_estimate=cost(feats * width, feats * width * 6),
    )(after, shares)
    return features, grad_weight


def solution(mesh):
    placed = (
        P(("col", "row"), None),
        P(("col", "row"), None),
        P(("col", "row"), "depth"),
        P("depth", None),
        P("row", "col", None, None, None),
        P("row", "col", None),
        P("row", "col", None),
        P("row", "col"),
    )
    return jax.shard_map(
        shards,
        mesh=mesh,
        in_specs=placed,
        out_specs=(P(("row", "col"), "depth"), P("depth", None)),
        check_vma=False,
    )
```

```python
import functools

import jax
import jax.numpy as jnp
from jax import lax
from jax.experimental import pallas as pl
from jax.experimental.pallas import tpu as pltpu
from jax.sharding import PartitionSpec as P

LANES = 128
GROUP = 8
CHUNK = 16
PAIR = 2
VMEM = pl.BlockSpec(memory_space=pltpu.VMEM)
SMEM = pl.BlockSpec(memory_space=pltpu.SMEM)
HBM = pl.BlockSpec(memory_space=pltpu.HBM)
ANY = pl.BlockSpec(memory_space=pl.ANY)


def params(mib):
    return pltpu.CompilerParams(vmem_limit_bytes=int(mib * 2**20))


def cost(flops, moved):
    return pl.CostEstimate(flops=flops, bytes_accessed=moved, transcendentals=0)


def panel_kernel(
    grad_hbm, mask_hbm, weight_hbm, panel_ref, after_ref, grad, mask, weight, arrived
):
    after_ref[...] = jnp.zeros_like(after_ref)
    copies = [
        pltpu.make_async_copy(mask_hbm, mask, arrived.at[0]),
        pltpu.make_async_copy(grad_hbm, grad, arrived.at[1]),
        pltpu.make_async_copy(weight_hbm, weight, arrived.at[2]),
    ]
    for copy in copies:
        copy.start()
    for copy in copies:
        copy.wait()
    masked = grad[...] * mask[...].astype(jnp.float32).astype(jnp.bfloat16)
    panel_ref[...] = lax.dot_general(
        masked, weight[...], (((1,), (1,)), ((), ())), preferred_element_type=jnp.float32
    ).astype(jnp.bfloat16)


def weight_kernel(
    grad_hbm, mask_hbm, aggregated_hbm, before_ref, out_ref, after_ref, grad, mask, aggregated, arrived
):
    copies = [
        pltpu.make_async_copy(mask_hbm, mask, arrived.at[0]),
        pltpu.make_async_copy(grad_hbm, grad, arrived.at[1]),
        pltpu.make_async_copy(aggregated_hbm, aggregated, arrived.at[2]),
    ]
    for copy in copies:
        copy.start()
    for copy in copies:
        copy.wait()
    after_ref[...] = jnp.zeros_like(after_ref)
    flipped = aggregated[...].T
    feats = flipped.shape[0]
    for j in range(grad.shape[1] // LANES):
        part = slice(j * LANES, (j + 1) * LANES)
        masked = grad[:, part] * mask[:, part].astype(jnp.float32).astype(jnp.bfloat16)
        term = jnp.dot(flipped, masked, preferred_element_type=jnp.float32)
        out_ref[j * feats : (j + 1) * feats, :] = term.astype(jnp.bfloat16)


def pack_kernel(after_ref, near, four, packed_ref):
    nodes = near.shape[0]
    packed_ref[0:nodes, :] = near[...]
    packed_ref[nodes : 2 * nodes, :] = four[...]


def sum_kernel(pieces, sent_in, spread_ref, sent_out, piece_ref):
    rows, lanes = spread_ref.shape
    terms = spread_ref[...].astype(jnp.float32).reshape(pieces, rows // pieces, lanes)
    piece_ref[...] = jnp.sum(terms, axis=0)


def tiles_kernel(
    live_ref, row_ref, col_ref, tiles_hbm, near, four, got_1, got_2, got_3, out_ref,
    tiles, panel, total, arrived,
):
    slots, size = tiles.shape[0], tiles.shape[1]
    copies = []
    for k in range(slots // CHUNK):
        part = pl.ds(k * CHUNK, CHUNK)
        copies.append(pltpu.make_async_copy(tiles_hbm.at[part], tiles.at[part], arrived.at[k]))
        copies[-1].start()
    total[...] = jnp.zeros_like(total)
    place = 0
    for part in (near, four, got_1, got_2, got_3):
        for k in range(part.shape[0] // size):
            panel[place] = part[k * size : (k + 1) * size, :]
            place += 1
    live = live_ref[0]

    def group(g, carry):
        first = g * GROUP
        terms = []
        for u in range(GROUP):
            terms.append(
                jnp.dot(
                    tiles[first + u], panel[col_ref[first + u]], preferred_element_type=jnp.float32
                )
            )
        for u in range(GROUP):
            r = row_ref[first + u]
            total[r] = total[r] + terms[u]
        return carry

    for k in range(slots // CHUNK):
        copies[k].wait()
        last = jnp.minimum((k + 1) * CHUNK, live)
        lax.fori_loop(k * CHUNK // GROUP, (last + GROUP - 1) // GROUP, group, 0)
    owners, height = out_ref.shape[0], out_ref.shape[1]
    for c in range(owners):
        for k in range(height // size):
            out_ref[c, k * size : (k + 1) * size, :] = total[c * (height // size) + k].astype(
                jnp.bfloat16
            )


def halves_kernel(half_ref, got_ref, keep_ref, send_ref, total):
    owners, height = got_ref.shape[0], got_ref.shape[1]
    for k in range(height // LANES):
        rows = slice(k * LANES, (k + 1) * LANES)
        acc = got_ref[0, rows, :].astype(jnp.float32)
        for c in range(1, owners):
            acc = acc + got_ref[c, rows, :].astype(jnp.float32)
        total[rows, :] = acc
    own = keep_ref.shape[0]
    half = half_ref[0]
    keep_ref[...] = total[pl.ds(pl.multiple_of(half * own, own), own), :]
    send_ref[...] = total[pl.ds(pl.multiple_of((1 - half) * own, own), own), :].astype(jnp.bfloat16)


def share_kernel(after_ref, piece_ref, out_ref):
    rows, lanes = out_ref.shape
    piece = piece_ref[...]
    repeated = jnp.broadcast_to(piece[None], (rows // piece.shape[0],) + piece.shape)
    out_ref[...] = repeated.reshape(rows, lanes).astype(jnp.bfloat16)


def features_kernel(keep_ref, got_ref, features_ref, after_ref):
    after_ref[...] = jnp.zeros_like(after_ref)
    features_ref[...] = (keep_ref[...] + got_ref[...].astype(jnp.float32)).astype(jnp.bfloat16)


def spread_kernel(after_ref, shares_ref, weight_ref):
    feats = weight_ref.shape[0]
    for g in range(shares_ref.shape[0] // feats):
        weight_ref[:, g * LANES : (g + 1) * LANES] = shares_ref[
            g * feats : (g + 1) * feats, :
        ].astype(jnp.float32)


def shards(grad_out, relu_mask, aggregated, weight, adj_tiles, tile_row, tile_col, tile_count):
    n_row, n_col = lax.axis_size("row"), lax.axis_size("col")
    n_y = n_col // PAIR
    lines = [[y * PAIR + h for y in range(n_y)] for h in range(PAIR)]
    nodes, width = grad_out.shape
    feats = weight.shape[0]
    tile_data = adj_tiles[0, 0]
    slots, size = tile_data.shape[0], tile_data.shape[1]
    block_tiles = nodes * n_col // size
    per_owner = nodes // size
    bf, f32 = jnp.bfloat16, jnp.float32
    shape = jax.ShapeDtypeStruct
    token = shape((8, LANES), f32)

    def swap(value, mask):
        return lax.ppermute(value, "row", [(i, i ^ mask) for i in range(n_row)])

    def swap_pair(value):
        return lax.ppermute(value, "col", [(i, i ^ 1) for i in range(n_col)])

    def line_all_to_all(value):
        return lax.all_to_all(value, "col", 0, 0, axis_index_groups=lines, tiled=True)

    def grid_all_to_all(value):
        pieces = value.reshape(n_row * n_col, value.shape[0] // (n_row * n_col), LANES)
        return lax.all_to_all(pieces, ("row", "col"), 0, 0, tiled=True).reshape(value.shape)

    near, after = pl.pallas_call(
        panel_kernel,
        out_shape=(shape((nodes, feats), bf), token),
        in_specs=[HBM] * 3,
        out_specs=(VMEM, VMEM),
        scratch_shapes=[
            pltpu.VMEM((nodes, width), bf),
            pltpu.VMEM((nodes, width), jnp.int32),
            pltpu.VMEM((feats, width), bf),
            pltpu.SemaphoreType.DMA((3,)),
        ],
        compiler_params=params(53.75),
        cost_estimate=cost(2 * nodes * width * feats, nodes * width * 8),
    )(grad_out, relu_mask, weight)

    four = swap(near, 4)

    term, ready = pl.pallas_call(
        weight_kernel,
        out_shape=(shape((width // LANES * feats, LANES), bf), token),
        in_specs=[HBM] * 3 + [VMEM],
        out_specs=(VMEM, VMEM),
        scratch_shapes=[
            pltpu.VMEM((nodes, width), bf),
            pltpu.VMEM((nodes, width), jnp.int32),
            pltpu.VMEM((nodes, feats), bf),
            pltpu.SemaphoreType.DMA((3,)),
        ],
        compiler_params=params(53.75),
        cost_estimate=cost(2 * 10**10, nodes * width * 4),
    )(grad_out, relu_mask, aggregated, after)
    spread = grid_all_to_all(term)
    packed = pl.pallas_call(
        pack_kernel,
        out_shape=shape((2 * nodes, feats), bf),
        in_specs=[VMEM] * 3,
        out_specs=VMEM,
        compiler_params=params(16),
        cost_estimate=cost(nodes * feats, nodes * feats * 8),
    )(ready, near, four)
    got_1, got_2, got_3 = swap(packed, 1), swap(packed, 2), swap(packed, 3)

    live = tile_count[0, 0]
    away = (tile_col[0, 0] * size // nodes) ^ lax.axis_index("row")
    chunk = (away & 3) * 2 + (away >> 2)
    col_at = chunk * per_owner + tile_col[0, 0] % per_owner
    row_at = jnp.where(jnp.arange(slots, dtype=jnp.int32) < live, tile_row[0, 0], block_tiles)

    sent = pl.pallas_call(
        tiles_kernel,
        out_shape=shape((n_y, PAIR * nodes, feats), bf),
        in_specs=[SMEM] * 3 + [HBM] + [VMEM] * 5,
        out_specs=VMEM,
        scratch_shapes=[
            pltpu.VMEM((slots, size, size), bf),
            pltpu.VMEM((n_row * per_owner, size, feats), bf),
            pltpu.VMEM((block_tiles + 1, size, feats), f32),
            pltpu.SemaphoreType.DMA((slots // CHUNK,)),
        ],
        compiler_params=params(50),
        cost_estimate=cost(2 * 10**10, slots * size * size * 2),
    )(live.reshape(1), row_at, col_at, tile_data, near, four, got_1, got_2, got_3)
    sent, piece = pl.pallas_call(
        functools.partial(sum_kernel, n_row * n_col),
        out_shape=(
            shape(sent.shape, bf),
            shape((term.shape[0] // (n_row * n_col), LANES), f32),
        ),
        in_specs=[ANY, VMEM],
        out_specs=(ANY, VMEM),
        input_output_aliases={0: 0},
        compiler_params=params(16),
        cost_estimate=cost(term.size, term.size * 2),
    )(sent, spread)
    got = line_all_to_all(sent)

    half = (lax.axis_index("col") & (PAIR - 1)).astype(jnp.int32).reshape(1)
    keep, send = pl.pallas_call(
        halves_kernel,
        out_shape=(shape((nodes, feats), f32), shape((nodes, feats), bf)),
        in_specs=[SMEM, VMEM],
        out_specs=(VMEM, VMEM),
        scratch_shapes=[pltpu.VMEM((PAIR * nodes, feats), f32)],
        compiler_params=params(16),
        cost_estimate=cost(nodes * feats * n_col, nodes * feats * n_col * 2),
    )(half, got)
    other = swap_pair(send)
    whole = pl.pallas_call(
        share_kernel,
        out_shape=shape(term.shape, bf),
        in_specs=[ANY, VMEM],
        out_specs=VMEM,
        compiler_params=params(16),
        cost_estimate=cost(2 * 10**10, term.size * 4),
    )(send, piece)
    shares = grid_all_to_all(whole)
    features, after = pl.pallas_call(
        features_kernel,
        out_shape=(shape((nodes, feats), bf), token),
        in_specs=[VMEM] * 2,
        out_specs=(VMEM, VMEM),
        compiler_params=params(16),
        cost_estimate=cost(2 * 10**10, nodes * feats * 4),
    )(keep, other)
    grad_weight = pl.pallas_call(
        spread_kernel,
        out_shape=shape((feats, width), f32),
        in_specs=[ANY, VMEM],
        out_specs=VMEM,
        compiler_params=params(16),
        cost_estimate=cost(feats * width, feats * width * 6),
    )(after, shares)
    return features, grad_weight


def solution(mesh):
    placed = (
        P(("col", "row"), None),
        P(("col", "row"), None),
        P(("col", "row"), "depth"),
        P("depth", None),
        P("row", "col", None, None, None),
        P("row", "col", None),
        P("row", "col", None),
        P("row", "col"),
    )
    return jax.shard_map(
        shards,
        mesh=mesh,
        in_specs=placed,
        out_specs=(P(("row", "col"), "depth"), P("depth", None)),
        check_vma=False,
    )
```

```python
import jax
import jax.numpy as jnp
from jax import lax
from jax.experimental import pallas as pl
from jax.experimental.pallas import tpu as pltpu
from jax.sharding import PartitionSpec as P

LANES = 128
GROUP = 8
CHUNK = 16
PAIR = 2
VMEM = pl.BlockSpec(memory_space=pltpu.VMEM)
SMEM = pl.BlockSpec(memory_space=pltpu.SMEM)
HBM = pl.BlockSpec(memory_space=pl.ANY)


def params(mib):
    return pltpu.CompilerParams(vmem_limit_bytes=int(mib * 2**20))


def cost(flops, moved):
    return pl.CostEstimate(flops=flops, bytes_accessed=moved, transcendentals=0)


def panel_kernel(
    grad_hbm, mask_hbm, weight_hbm, panel_ref, after_ref, grad, mask, weight, arrived
):
    after_ref[...] = jnp.zeros_like(after_ref)
    copies = [
        pltpu.make_async_copy(mask_hbm, mask, arrived.at[0]),
        pltpu.make_async_copy(grad_hbm, grad, arrived.at[1]),
        pltpu.make_async_copy(weight_hbm, weight, arrived.at[2]),
    ]
    for copy in copies:
        copy.start()
    for copy in copies:
        copy.wait()
    masked = grad[...] * mask[...].astype(jnp.float32).astype(jnp.bfloat16)
    panel_ref[...] = lax.dot_general(
        masked, weight[...], (((1,), (1,)), ((), ())), preferred_element_type=jnp.float32
    ).astype(jnp.bfloat16)


def weight_kernel(
    grad_hbm, mask_hbm, aggregated_hbm, before_ref, out_ref, after_ref, grad, mask, aggregated, arrived
):
    copies = [
        pltpu.make_async_copy(mask_hbm, mask, arrived.at[0]),
        pltpu.make_async_copy(grad_hbm, grad, arrived.at[1]),
        pltpu.make_async_copy(aggregated_hbm, aggregated, arrived.at[2]),
    ]
    for copy in copies:
        copy.start()
    for copy in copies:
        copy.wait()
    after_ref[...] = jnp.zeros_like(after_ref)
    flipped = aggregated[...].T
    feats = flipped.shape[0]
    for j in range(grad.shape[1] // LANES):
        part = slice(j * LANES, (j + 1) * LANES)
        masked = grad[:, part] * mask[:, part].astype(jnp.float32).astype(jnp.bfloat16)
        term = jnp.dot(flipped, masked, preferred_element_type=jnp.float32)
        out_ref[j * feats : (j + 1) * feats, :] = term.astype(jnp.bfloat16)


def pack_kernel(after_ref, near, four, packed_ref):
    nodes = near.shape[0]
    packed_ref[0:nodes, :] = near[...]
    packed_ref[nodes : 2 * nodes, :] = four[...]


def sum_kernel(after_ref, spread_ref, out_ref):
    acc = spread_ref[0].astype(jnp.float32)
    for c in range(1, spread_ref.shape[0]):
        acc = acc + spread_ref[c].astype(jnp.float32)
    out_ref[...] = acc.astype(jnp.bfloat16)


def quarter_kernel(sent_in, own, row_1, row_2, row_3, sent_out, out_ref):
    f32 = jnp.float32
    total = (own[...].astype(f32) + row_1[...].astype(f32)) + (
        row_2[...].astype(f32) + row_3[...].astype(f32)
    )
    out_ref[...] = total.astype(jnp.bfloat16)


def tiles_kernel(
    live_ref, row_ref, col_ref, tiles_hbm, near, four, got_1, got_2, got_3, out_hbm,
    tiles, panel, total, done, arrived, written,
):
    slots, size = tiles.shape[0], tiles.shape[1]
    copies = []
    for k in range(slots // CHUNK):
        part = pl.ds(k * CHUNK, CHUNK)
        copies.append(pltpu.make_async_copy(tiles_hbm.at[part], tiles.at[part], arrived.at[k]))
        copies[-1].start()
    total[...] = jnp.zeros_like(total)
    place = 0
    for part in (near, four, got_1, got_2, got_3):
        for k in range(part.shape[0] // size):
            panel[place] = part[k * size : (k + 1) * size, :]
            place += 1
    live = live_ref[0]

    def group(g, carry):
        first = g * GROUP
        terms = []
        for u in range(GROUP):
            terms.append(
                jnp.dot(
                    tiles[first + u], panel[col_ref[first + u]], preferred_element_type=jnp.float32
                )
            )
        for u in range(GROUP):
            r = row_ref[first + u]
            total[r] = total[r] + terms[u]
        return carry

    for k in range(slots // CHUNK):
        copies[k].wait()
        last = jnp.minimum((k + 1) * CHUNK, live)
        lax.fori_loop(k * CHUNK // GROUP, (last + GROUP - 1) // GROUP, group, 0)
    owners, height = done.shape[0], done.shape[1]
    results = []
    for c in range(owners):
        for k in range(height // size):
            done[c, k * size : (k + 1) * size, :] = total[c * (height // size) + k].astype(
                jnp.bfloat16
            )
        results.append(pltpu.make_async_copy(done.at[c], out_hbm.at[c], written.at[c]))
        results[-1].start()
    for result in results:
        result.wait()


def halves_kernel(half_ref, got_ref, keep_ref, send_ref, total):
    owners, height = got_ref.shape[0], got_ref.shape[1]
    for k in range(height // LANES):
        rows = slice(k * LANES, (k + 1) * LANES)
        acc = got_ref[0, rows, :].astype(jnp.float32)
        for c in range(1, owners):
            acc = acc + got_ref[c, rows, :].astype(jnp.float32)
        total[rows, :] = acc
    own = keep_ref.shape[0]
    half = half_ref[0]
    keep_ref[...] = total[pl.ds(pl.multiple_of(half * own, own), own), :]
    send_ref[...] = total[pl.ds(pl.multiple_of((1 - half) * own, own), own), :].astype(jnp.bfloat16)


def share_kernel(after_ref, own, got_4, got_pair, got_both, out_ref):
    f32 = jnp.float32
    total = (own[...].astype(f32) + got_4[...].astype(f32)) + (
        got_pair[...].astype(f32) + got_both[...].astype(f32)
    )
    total = total.astype(jnp.bfloat16)
    for c in range(out_ref.shape[0]):
        out_ref[c] = total


def features_kernel(keep_ref, got_ref, features_ref, after_ref):
    after_ref[...] = jnp.zeros_like(after_ref)
    features_ref[...] = (keep_ref[...] + got_ref[...].astype(jnp.float32)).astype(jnp.bfloat16)


def spread_kernel(after_ref, shares_ref, weight_ref):
    owners, rows = shares_ref.shape[0], shares_ref.shape[1]
    feats = weight_ref.shape[0]
    for g in range(owners * rows // feats):
        c, at = g * feats // rows, g * feats % rows
        weight_ref[:, g * LANES : (g + 1) * LANES] = shares_ref[c, at : at + feats, :].astype(
            jnp.float32
        )


def shards(grad_out, relu_mask, aggregated, weight, adj_tiles, tile_row, tile_col, tile_count):
    n_row, n_col = lax.axis_size("row"), lax.axis_size("col")
    n_y = n_col // PAIR
    lines = [[y * PAIR + h for y in range(n_y)] for h in range(PAIR)]
    nodes, width = grad_out.shape
    feats = weight.shape[0]
    tile_data = adj_tiles[0, 0]
    slots, size = tile_data.shape[0], tile_data.shape[1]
    block_tiles = nodes * n_col // size
    per_owner = nodes // size
    bf, f32 = jnp.bfloat16, jnp.float32
    shape = jax.ShapeDtypeStruct
    token = shape((8, LANES), f32)

    def swap(value, mask):
        return lax.ppermute(value, "row", [(i, i ^ mask) for i in range(n_row)])

    def swap_pair(value, mask=0):
        if mask == 0:
            return lax.ppermute(value, "col", [(i, i ^ 1) for i in range(n_col)])
        count = n_row * n_col
        return lax.ppermute(
            value, ("row", "col"), [(i, i ^ (mask * n_col + 1)) for i in range(count)]
        )

    def line_all_to_all(value):
        return lax.all_to_all(value, "col", 0, 0, axis_index_groups=lines, tiled=True)

    near, first = pl.pallas_call(
        panel_kernel,
        out_shape=(shape((nodes, feats), bf), token),
        in_specs=[HBM] * 3,
        out_specs=(VMEM, VMEM),
        scratch_shapes=[
            pltpu.VMEM((nodes, width), bf),
            pltpu.VMEM((nodes, width), jnp.int32),
            pltpu.VMEM((feats, width), bf),
            pltpu.SemaphoreType.DMA((3,)),
        ],
        compiler_params=params(53.75),
        cost_estimate=cost(2 * nodes * width * feats, nodes * width * 8),
    )(grad_out, relu_mask, weight)

    four = swap(near, 4)

    term, ready = pl.pallas_call(
        weight_kernel,
        out_shape=(shape((width // LANES * feats, LANES), bf), token),
        in_specs=[HBM] * 3 + [VMEM],
        out_specs=(VMEM, VMEM),
        scratch_shapes=[
            pltpu.VMEM((nodes, width), bf),
            pltpu.VMEM((nodes, width), jnp.int32),
            pltpu.VMEM((nodes, feats), bf),
            pltpu.SemaphoreType.DMA((3,)),
        ],
        compiler_params=params(53.75),
        cost_estimate=cost(2 * 10**10, nodes * width * 4),
    )(grad_out, relu_mask, aggregated, first)
    spread = line_all_to_all(term.reshape(n_y, term.shape[0] // n_y, LANES))
    extra = spread.shape[1]
    packed = pl.pallas_call(
        pack_kernel,
        out_shape=shape((2 * nodes, feats), bf),
        in_specs=[VMEM] * 3,
        out_specs=VMEM,
        compiler_params=params(16),
        cost_estimate=cost(2 * 10**10, nodes * feats * 8),
    )(ready, near, four)
    got_1, got_2, got_3 = swap(packed, 1), swap(packed, 2), swap(packed, 3)

    share = pl.pallas_call(
        sum_kernel,
        out_shape=shape((extra, LANES), bf),
        in_specs=[HBM, VMEM],
        out_specs=VMEM,
        compiler_params=params(16),
        cost_estimate=cost(n_y * extra * LANES, n_y * extra * LANES * 2),
    )(packed, spread)
    row_1, row_2, row_3 = swap(share, 1), swap(share, 2), swap(share, 3)

    live = tile_count[0, 0]
    away = (tile_col[0, 0] * size // nodes) ^ lax.axis_index("row")
    chunk = (away & 3) * 2 + (away >> 2)
    col_at = chunk * per_owner + tile_col[0, 0] % per_owner
    row_at = jnp.where(jnp.arange(slots, dtype=jnp.int32) < live, tile_row[0, 0], block_tiles)

    sent = pl.pallas_call(
        tiles_kernel,
        out_shape=shape((n_y, PAIR * nodes, feats), bf),
        in_specs=[SMEM] * 3 + [HBM] + [VMEM] * 5,
        out_specs=HBM,
        scratch_shapes=[
            pltpu.VMEM((slots, size, size), bf),
            pltpu.VMEM((n_row * per_owner, size, feats), bf),
            pltpu.VMEM((block_tiles + 1, size, feats), f32),
            pltpu.VMEM((n_y, PAIR * nodes, feats), bf),
            pltpu.SemaphoreType.DMA((slots // CHUNK,)),
            pltpu.SemaphoreType.DMA((n_y,)),
        ],
        compiler_params=params(50),
        cost_estimate=cost(2 * 10**10, slots * size * size * 2),
    )(live.reshape(1), row_at, col_at, tile_data, near, four, got_1, got_2, got_3)
    sent, share = pl.pallas_call(
        quarter_kernel,
        out_shape=(shape(sent.shape, bf), shape((extra, LANES), bf)),
        in_specs=[HBM] + [VMEM] * 4,
        out_specs=(HBM, VMEM),
        input_output_aliases={0: 0},
        compiler_params=params(16),
        cost_estimate=cost(4 * extra * LANES, 4 * extra * LANES * 2),
    )(sent, share, row_1, row_2, row_3)
    got = line_all_to_all(sent)
    far_4, far_pair, far_both = swap(share, 4), swap_pair(share), swap_pair(share, 4)

    half = (lax.axis_index("col") & (PAIR - 1)).astype(jnp.int32).reshape(1)
    keep, send = pl.pallas_call(
        halves_kernel,
        out_shape=(shape((nodes, feats), f32), shape((nodes, feats), bf)),
        in_specs=[SMEM, VMEM],
        out_specs=(VMEM, VMEM),
        scratch_shapes=[pltpu.VMEM((PAIR * nodes, feats), f32)],
        compiler_params=params(16),
        cost_estimate=cost(nodes * feats * n_col, nodes * feats * n_col * 2),
    )(half, got)
    other = swap_pair(send)
    whole = pl.pallas_call(
        share_kernel,
        out_shape=shape((n_y, extra, LANES), bf),
        in_specs=[HBM] + [VMEM] * 4,
        out_specs=VMEM,
        compiler_params=params(16),
        cost_estimate=cost(2 * 10**10, n_y * extra * LANES * 2),
    )(send, share, far_4, far_pair, far_both)
    shares = line_all_to_all(whole)
    features, after = pl.pallas_call(
        features_kernel,
        out_shape=(shape((nodes, feats), bf), token),
        in_specs=[VMEM] * 2,
        out_specs=(VMEM, VMEM),
        compiler_params=params(16),
        cost_estimate=cost(2 * 10**10, nodes * feats * 4),
    )(keep, other)
    grad_weight = pl.pallas_call(
        spread_kernel,
        out_shape=shape((feats, width), f32),
        in_specs=[HBM, VMEM],
        out_specs=VMEM,
        compiler_params=params(16),
        cost_estimate=cost(feats * width, feats * width * 6),
    )(after, shares)
    return features, grad_weight


def solution(mesh):
    placed = (
        P(("col", "row"), None),
        P(("col", "row"), None),
        P(("col", "row"), "depth"),
        P("depth", None),
        P("row", "col", None, None, None),
        P("row", "col", None),
        P("row", "col", None),
        P("row", "col"),
    )
    return jax.shard_map(
        shards,
        mesh=mesh,
        in_specs=placed,
        out_specs=(P(("row", "col"), "depth"), P("depth", None)),
        check_vma=False,
    )
```

```python
import jax
import jax.numpy as jnp
from jax import lax
from jax.experimental import pallas as pl
from jax.experimental.pallas import tpu as pltpu
from jax.sharding import PartitionSpec as P

LANES = 128
GROUP = 8
CHUNK = 16
PAIR = 2
VMEM = pl.BlockSpec(memory_space=pltpu.VMEM)
SMEM = pl.BlockSpec(memory_space=pltpu.SMEM)
HBM = pl.BlockSpec(memory_space=pl.ANY)


def params(mib):
    return pltpu.CompilerParams(vmem_limit_bytes=int(mib * 2**20))


def cost(flops, moved):
    return pl.CostEstimate(flops=flops, bytes_accessed=moved, transcendentals=0)


def panel_kernel(
    grad_hbm, mask_hbm, weight_hbm, panel_ref, after_ref, grad, mask, weight, arrived
):
    after_ref[...] = jnp.zeros_like(after_ref)
    copies = [
        pltpu.make_async_copy(mask_hbm, mask, arrived.at[0]),
        pltpu.make_async_copy(grad_hbm, grad, arrived.at[1]),
        pltpu.make_async_copy(weight_hbm, weight, arrived.at[2]),
    ]
    for copy in copies:
        copy.start()
    for copy in copies:
        copy.wait()
    masked = grad[...] * mask[...].astype(jnp.float32).astype(jnp.bfloat16)
    panel_ref[...] = lax.dot_general(
        masked, weight[...], (((1,), (1,)), ((), ())), preferred_element_type=jnp.float32
    ).astype(jnp.bfloat16)


def weight_kernel(
    grad_hbm, mask_hbm, aggregated_hbm, before_ref, out_ref, after_ref, grad, mask, aggregated, arrived
):
    copies = [
        pltpu.make_async_copy(mask_hbm, mask, arrived.at[0]),
        pltpu.make_async_copy(grad_hbm, grad, arrived.at[1]),
        pltpu.make_async_copy(aggregated_hbm, aggregated, arrived.at[2]),
    ]
    for copy in copies:
        copy.start()
    for copy in copies:
        copy.wait()
    after_ref[...] = jnp.zeros_like(after_ref)
    flipped = aggregated[...].T
    feats = flipped.shape[0]
    for j in range(grad.shape[1] // LANES):
        part = slice(j * LANES, (j + 1) * LANES)
        masked = grad[:, part] * mask[:, part].astype(jnp.float32).astype(jnp.bfloat16)
        term = jnp.dot(flipped, masked, preferred_element_type=jnp.float32)
        out_ref[j * feats : (j + 1) * feats, :] = term.astype(jnp.bfloat16)


def pack_kernel(after_ref, near, four, packed_ref):
    nodes = near.shape[0]
    packed_ref[0:nodes, :] = near[...]
    packed_ref[nodes : 2 * nodes, :] = four[...]


def sum_kernel(after_ref, spread_ref, out_ref):
    acc = spread_ref[0].astype(jnp.float32)
    for c in range(1, spread_ref.shape[0]):
        acc = acc + spread_ref[c].astype(jnp.float32)
    out_ref[...] = acc.astype(jnp.bfloat16)


def pair_kernel(sent_in, own, other, sent_out, out_ref):
    total = own[...].astype(jnp.float32) + other[...].astype(jnp.float32)
    out_ref[...] = total.astype(jnp.bfloat16)


def tiles_kernel(
    live_ref, row_ref, col_ref, tiles_hbm, near, four, got_1, got_2, got_3, out_hbm,
    tiles, panel, total, done, arrived, written,
):
    slots, size = tiles.shape[0], tiles.shape[1]
    copies = []
    for k in range(slots // CHUNK):
        part = pl.ds(k * CHUNK, CHUNK)
        copies.append(pltpu.make_async_copy(tiles_hbm.at[part], tiles.at[part], arrived.at[k]))
        copies[-1].start()
    total[...] = jnp.zeros_like(total)
    place = 0
    for part in (near, four, got_1, got_2, got_3):
        for k in range(part.shape[0] // size):
            panel[place] = part[k * size : (k + 1) * size, :]
            place += 1
    live = live_ref[0]

    def group(g, carry):
        first = g * GROUP
        terms = []
        for u in range(GROUP):
            terms.append(
                jnp.dot(
                    tiles[first + u], panel[col_ref[first + u]], preferred_element_type=jnp.float32
                )
            )
        for u in range(GROUP):
            r = row_ref[first + u]
            total[r] = total[r] + terms[u]
        return carry

    for k in range(slots // CHUNK):
        copies[k].wait()
        last = jnp.minimum((k + 1) * CHUNK, live)
        lax.fori_loop(k * CHUNK // GROUP, (last + GROUP - 1) // GROUP, group, 0)
    owners, height = done.shape[0], done.shape[1]
    results = []
    for c in range(owners):
        for k in range(height // size):
            done[c, k * size : (k + 1) * size, :] = total[c * (height // size) + k].astype(
                jnp.bfloat16
            )
        results.append(pltpu.make_async_copy(done.at[c], out_hbm.at[c], written.at[c]))
        results[-1].start()
    for result in results:
        result.wait()


def halves_kernel(half_ref, got_ref, keep_ref, send_ref, total):
    owners, height = got_ref.shape[0], got_ref.shape[1]
    for k in range(height // LANES):
        rows = slice(k * LANES, (k + 1) * LANES)
        acc = got_ref[0, rows, :].astype(jnp.float32)
        for c in range(1, owners):
            acc = acc + got_ref[c, rows, :].astype(jnp.float32)
        total[rows, :] = acc
    own = keep_ref.shape[0]
    half = half_ref[0]
    keep_ref[...] = total[pl.ds(pl.multiple_of(half * own, own), own), :]
    send_ref[...] = total[pl.ds(pl.multiple_of((1 - half) * own, own), own), :].astype(jnp.bfloat16)


def share_kernel(after_ref, own, other, out_ref):
    total = own[...].astype(jnp.float32) + other[...].astype(jnp.float32)
    total = total.astype(jnp.bfloat16)
    for c in range(out_ref.shape[0]):
        out_ref[c] = total


def features_kernel(keep_ref, got_ref, features_ref, after_ref):
    after_ref[...] = jnp.zeros_like(after_ref)
    features_ref[...] = (keep_ref[...] + got_ref[...].astype(jnp.float32)).astype(jnp.bfloat16)


def spread_kernel(after_ref, shares_ref, weight_ref):
    owners, rows = shares_ref.shape[0], shares_ref.shape[1]
    feats = weight_ref.shape[0]
    for g in range(owners * rows // feats):
        c, at = g * feats // rows, g * feats % rows
        weight_ref[:, g * LANES : (g + 1) * LANES] = shares_ref[c, at : at + feats, :].astype(
            jnp.float32
        )


def shards(grad_out, relu_mask, aggregated, weight, adj_tiles, tile_row, tile_col, tile_count):
    n_row, n_col = lax.axis_size("row"), lax.axis_size("col")
    n_y = n_col // PAIR
    lines = [[y * PAIR + h for y in range(n_y)] for h in range(PAIR)]
    nodes, width = grad_out.shape
    feats = weight.shape[0]
    tile_data = adj_tiles[0, 0]
    slots, size = tile_data.shape[0], tile_data.shape[1]
    block_tiles = nodes * n_col // size
    per_owner = nodes // size
    bf, f32 = jnp.bfloat16, jnp.float32
    shape = jax.ShapeDtypeStruct
    token = shape((8, LANES), f32)

    def swap(value, mask):
        return lax.ppermute(value, "row", [(i, i ^ mask) for i in range(n_row)])

    def swap_pair(value):
        return lax.ppermute(value, "col", [(i, i ^ 1) for i in range(n_col)])

    def line_all_to_all(value):
        return lax.all_to_all(value, "col", 0, 0, axis_index_groups=lines, tiled=True)

    near, first = pl.pallas_call(
        panel_kernel,
        out_shape=(shape((nodes, feats), bf), token),
        in_specs=[HBM] * 3,
        out_specs=(VMEM, VMEM),
        scratch_shapes=[
            pltpu.VMEM((nodes, width), bf),
            pltpu.VMEM((nodes, width), jnp.int32),
            pltpu.VMEM((feats, width), bf),
            pltpu.SemaphoreType.DMA((3,)),
        ],
        compiler_params=params(53.75),
        cost_estimate=cost(2 * nodes * width * feats, nodes * width * 8),
    )(grad_out, relu_mask, weight)

    four = swap(near, 4)

    term, ready = pl.pallas_call(
        weight_kernel,
        out_shape=(shape((width // LANES * feats, LANES), bf), token),
        in_specs=[HBM] * 3 + [VMEM],
        out_specs=(VMEM, VMEM),
        scratch_shapes=[
            pltpu.VMEM((nodes, width), bf),
            pltpu.VMEM((nodes, width), jnp.int32),
            pltpu.VMEM((nodes, feats), bf),
            pltpu.SemaphoreType.DMA((3,)),
        ],
        compiler_params=params(53.9),
        cost_estimate=cost(2 * 10**10, nodes * width * 4),
    )(grad_out, relu_mask, aggregated, first)
    spread = line_all_to_all(term.reshape(n_y, term.shape[0] // n_y, LANES))
    extra = spread.shape[1]
    packed = pl.pallas_call(
        pack_kernel,
        out_shape=shape((2 * nodes, feats), bf),
        in_specs=[VMEM] * 3,
        out_specs=VMEM,
        compiler_params=params(16),
        cost_estimate=cost(2 * 10**10, nodes * feats * 8),
    )(ready, near, four)
    got_1, got_2, got_3 = swap(packed, 1), swap(packed, 2), swap(packed, 3)

    share = pl.pallas_call(
        sum_kernel,
        out_shape=shape((extra, LANES), bf),
        in_specs=[HBM, VMEM],
        out_specs=VMEM,
        compiler_params=params(16),
        cost_estimate=cost(2 * 10**10, n_y * extra * LANES * 2),
    )(packed, spread)
    row_1 = swap(share, 1)

    live = tile_count[0, 0]
    away = (tile_col[0, 0] * size // nodes) ^ lax.axis_index("row")
    chunk = (away & 3) * 2 + (away >> 2)
    col_at = chunk * per_owner + tile_col[0, 0] % per_owner
    row_at = jnp.where(jnp.arange(slots, dtype=jnp.int32) < live, tile_row[0, 0], block_tiles)

    sent = pl.pallas_call(
        tiles_kernel,
        out_shape=shape((n_y, PAIR * nodes, feats), bf),
        in_specs=[SMEM] * 3 + [HBM] + [VMEM] * 5,
        out_specs=HBM,
        scratch_shapes=[
            pltpu.VMEM((slots, size, size), bf),
            pltpu.VMEM((n_row * per_owner, size, feats), bf),
            pltpu.VMEM((block_tiles + 1, size, feats), f32),
            pltpu.VMEM((n_y, PAIR * nodes, feats), bf),
            pltpu.SemaphoreType.DMA((slots // CHUNK,)),
            pltpu.SemaphoreType.DMA((n_y,)),
        ],
        compiler_params=params(50),
        cost_estimate=cost(2 * 10**10, slots * size * size * 2),
    )(live.reshape(1), row_at, col_at, tile_data, near, four, got_1, got_2, got_3)
    sent, share = pl.pallas_call(
        pair_kernel,
        out_shape=(shape(sent.shape, bf), shape((extra, LANES), bf)),
        in_specs=[HBM] + [VMEM] * 2,
        out_specs=(HBM, VMEM),
        input_output_aliases={0: 0},
        compiler_params=params(16),
        cost_estimate=cost(4 * extra * LANES, 4 * extra * LANES * 2),
    )(sent, share, row_1)
    got = line_all_to_all(sent)
    for mask in (2, 4):
        share = (share.astype(f32) + swap(share, mask).astype(f32)).astype(bf)
    far = swap_pair(share)

    half = (lax.axis_index("col") & (PAIR - 1)).astype(jnp.int32).reshape(1)
    keep, send = pl.pallas_call(
        halves_kernel,
        out_shape=(shape((nodes, feats), f32), shape((nodes, feats), bf)),
        in_specs=[SMEM, VMEM],
        out_specs=(VMEM, VMEM),
        scratch_shapes=[pltpu.VMEM((PAIR * nodes, feats), f32)],
        compiler_params=params(16),
        cost_estimate=cost(nodes * feats * n_col, nodes * feats * n_col * 2),
    )(half, got)
    other = swap_pair(send)
    whole = pl.pallas_call(
        share_kernel,
        out_shape=shape((n_y, extra, LANES), bf),
        in_specs=[HBM] + [VMEM] * 2,
        out_specs=VMEM,
        compiler_params=params(16),
        cost_estimate=cost(2 * 10**10, n_y * extra * LANES * 2),
    )(send, share, far)
    shares = line_all_to_all(whole)
    features, after = pl.pallas_call(
        features_kernel,
        out_shape=(shape((nodes, feats), bf), token),
        in_specs=[VMEM] * 2,
        out_specs=(VMEM, VMEM),
        compiler_params=params(16),
        cost_estimate=cost(2 * 10**10, nodes * feats * 4),
    )(keep, other)
    grad_weight = pl.pallas_call(
        spread_kernel,
        out_shape=shape((feats, width), f32),
        in_specs=[HBM, VMEM],
        out_specs=VMEM,
        compiler_params=params(16),
        cost_estimate=cost(feats * width, feats * width * 6),
    )(after, shares)
    return features, grad_weight


def solution(mesh):
    placed = (
        P(("col", "row"), None),
        P(("col", "row"), None),
        P(("col", "row"), "depth"),
        P("depth", None),
        P("row", "col", None, None, None),
        P("row", "col", None),
        P("row", "col", None),
        P("row", "col"),
    )
    return jax.shard_map(
        shards,
        mesh=mesh,
        in_specs=placed,
        out_specs=(P(("row", "col"), "depth"), P("depth", None)),
        check_vma=False,
    )
```

```python
import functools

import jax
import jax.numpy as jnp
from jax import lax
from jax.experimental import pallas as pl
from jax.experimental.pallas import tpu as pltpu
from jax.sharding import PartitionSpec as P

LANES = 128
GROUP = 4
CHUNK = 16
PAIR = 2
VMEM = pl.BlockSpec(memory_space=pltpu.VMEM)
SMEM = pl.BlockSpec(memory_space=pltpu.SMEM)
HBM = pl.BlockSpec(memory_space=pl.ANY)


def params(mib):
    return pltpu.CompilerParams(vmem_limit_bytes=int(mib * 2**20))


def cost(flops, moved):
    return pl.CostEstimate(flops=flops, bytes_accessed=moved, transcendentals=0)


def panel_kernel(
    grad_hbm, mask_hbm, weight_hbm, panel_ref, after_ref, grad, mask, weight, arrived
):
    after_ref[...] = jnp.zeros_like(after_ref)
    copies = [
        pltpu.make_async_copy(mask_hbm, mask, arrived.at[0]),
        pltpu.make_async_copy(grad_hbm, grad, arrived.at[1]),
        pltpu.make_async_copy(weight_hbm, weight, arrived.at[2]),
    ]
    for copy in copies:
        copy.start()
    for copy in copies:
        copy.wait()
    masked = grad[...] * mask[...].astype(jnp.float32).astype(jnp.bfloat16)
    panel_ref[...] = lax.dot_general(
        masked, weight[...], (((1,), (1,)), ((), ())), preferred_element_type=jnp.float32
    ).astype(jnp.bfloat16)


def weight_kernel(
    grad_hbm, mask_hbm, aggregated_hbm, before_ref, out_ref, after_ref, grad, mask, aggregated, arrived
):
    copies = [
        pltpu.make_async_copy(mask_hbm, mask, arrived.at[0]),
        pltpu.make_async_copy(grad_hbm, grad, arrived.at[1]),
        pltpu.make_async_copy(aggregated_hbm, aggregated, arrived.at[2]),
    ]
    for copy in copies:
        copy.start()
    for copy in copies:
        copy.wait()
    after_ref[...] = jnp.zeros_like(after_ref)
    flipped = aggregated[...].T
    feats = flipped.shape[0]
    for j in range(grad.shape[1] // LANES):
        part = slice(j * LANES, (j + 1) * LANES)
        masked = grad[:, part] * mask[:, part].astype(jnp.float32).astype(jnp.bfloat16)
        term = jnp.dot(flipped, masked, preferred_element_type=jnp.float32)
        out_ref[j * feats : (j + 1) * feats, :] = term.astype(jnp.bfloat16)


def pack_kernel(after_ref, near, four, packed_ref):
    nodes = near.shape[0]
    packed_ref[0:nodes, :] = near[...]
    packed_ref[nodes : 2 * nodes, :] = four[...]


def sum_kernel(after_ref, spread_ref, out_ref):
    acc = spread_ref[0].astype(jnp.float32)
    for c in range(1, spread_ref.shape[0]):
        acc = acc + spread_ref[c].astype(jnp.float32)
    out_ref[...] = acc.astype(jnp.bfloat16)


def pair_kernel(sent_in, own, other, sent_out, out_ref):
    total = own[...].astype(jnp.float32) + other[...].astype(jnp.float32)
    out_ref[...] = total.astype(jnp.bfloat16)


def prepare_kernel(
    blank, live_ref, row_ref, col_ref, after_ref,
    pairs_ref, order_ref, col_at_ref, row_at_ref, counts, places,
):
    block_rows = counts.shape[0]
    live = live_ref[0]
    for r in range(block_rows):
        counts[r] = 0
    for i in range(order_ref.shape[0]):
        order_ref[i] = 0
        col_at_ref[i] = blank
    for i in range(row_at_ref.shape[0]):
        row_at_ref[i] = block_rows

    def count(s, carry):
        r = row_ref[s]
        counts[r] = counts[r] + 1
        return carry

    lax.fori_loop(0, live, count, 0)
    used = 0
    for r in range(block_rows):
        places[r] = used
        used = used + ((counts[r] + 1) & -2)
    pairs_ref[0] = used >> 1

    def place(s, carry):
        r = row_ref[s]
        at = places[r]
        places[r] = at + 1
        order_ref[at] = s
        col_at_ref[at] = col_ref[s]
        row_at_ref[at >> 1] = r
        return carry

    lax.fori_loop(0, live, place, 0)


def tiles_kernel(
    live_ref, pairs_ref, order_ref, col_ref, row_ref, tiles_hbm, near, four, got_1, got_2, got_3,
    out_hbm, tiles, panel, total, done, arrived, written,
):
    slots, size = tiles.shape[0], tiles.shape[1]
    copies = []
    for k in range(slots // CHUNK):
        part = pl.ds(k * CHUNK, CHUNK)
        copies.append(pltpu.make_async_copy(tiles_hbm.at[part], tiles.at[part], arrived.at[k]))
        pl.when(k * CHUNK < live_ref[0])(copies[-1].start)
    total[...] = jnp.zeros_like(total)
    place = 0
    for part in (near, four, got_1, got_2, got_3):
        for k in range(part.shape[0] // size):
            panel[place] = part[k * size : (k + 1) * size, :]
            place += 1
    panel[place] = jnp.zeros(panel.shape[1:], jnp.bfloat16)
    for k in range(slots // CHUNK):
        pl.when(k * CHUNK < live_ref[0])(copies[k].wait)

    def group(g, carry):
        terms = []
        for u in range(GROUP):
            at = 2 * (g * GROUP + u)
            left = jnp.concatenate([tiles[order_ref[at]], tiles[order_ref[at + 1]]], axis=1)
            right = jnp.concatenate([panel[col_ref[at]], panel[col_ref[at + 1]]], axis=0)
            terms.append(jnp.dot(left, right, preferred_element_type=jnp.float32))
        for u in range(GROUP):
            r = row_ref[g * GROUP + u]
            total[r] = total[r] + terms[u]
        return carry

    lax.fori_loop(0, (pairs_ref[0] + GROUP - 1) // GROUP, group, 0)
    owners, height = done.shape[0], done.shape[1]
    results = []
    for c in range(owners):
        for k in range(height // size):
            done[c, k * size : (k + 1) * size, :] = total[c * (height // size) + k].astype(
                jnp.bfloat16
            )
        results.append(pltpu.make_async_copy(done.at[c], out_hbm.at[c], written.at[c]))
        results[-1].start()
    for result in results:
        result.wait()


def halves_kernel(half_ref, got_ref, keep_ref, send_ref, total):
    owners, height = got_ref.shape[0], got_ref.shape[1]
    for k in range(height // LANES):
        rows = slice(k * LANES, (k + 1) * LANES)
        acc = got_ref[0, rows, :].astype(jnp.float32)
        for c in range(1, owners):
            acc = acc + got_ref[c, rows, :].astype(jnp.float32)
        total[rows, :] = acc
    own = keep_ref.shape[0]
    half = half_ref[0]
    keep_ref[...] = total[pl.ds(pl.multiple_of(half * own, own), own), :]
    send_ref[...] = total[pl.ds(pl.multiple_of((1 - half) * own, own), own), :].astype(jnp.bfloat16)


def share_kernel(after_ref, own, other, out_ref):
    total = own[...].astype(jnp.float32) + other[...].astype(jnp.float32)
    total = total.astype(jnp.bfloat16)
    for c in range(out_ref.shape[0]):
        out_ref[c] = total


def features_kernel(keep_ref, got_ref, features_ref, after_ref):
    after_ref[...] = jnp.zeros_like(after_ref)
    features_ref[...] = (keep_ref[...] + got_ref[...].astype(jnp.float32)).astype(jnp.bfloat16)


def spread_kernel(after_ref, shares_ref, weight_ref):
    owners, rows = shares_ref.shape[0], shares_ref.shape[1]
    feats = weight_ref.shape[0]
    for g in range(owners * rows // feats):
        c, at = g * feats // rows, g * feats % rows
        weight_ref[:, g * LANES : (g + 1) * LANES] = shares_ref[c, at : at + feats, :].astype(
            jnp.float32
        )


def shards(grad_out, relu_mask, aggregated, weight, adj_tiles, tile_row, tile_col, tile_count):
    n_row, n_col = lax.axis_size("row"), lax.axis_size("col")
    n_y = n_col // PAIR
    lines = [[y * PAIR + h for y in range(n_y)] for h in range(PAIR)]
    nodes, width = grad_out.shape
    feats = weight.shape[0]
    tile_data = adj_tiles[0, 0]
    slots, size = tile_data.shape[0], tile_data.shape[1]
    block_tiles = nodes * n_col // size
    per_owner = nodes // size
    bf, f32 = jnp.bfloat16, jnp.float32
    shape = jax.ShapeDtypeStruct
    token = shape((8, LANES), f32)

    def swap(value, mask):
        return lax.ppermute(value, "row", [(i, i ^ mask) for i in range(n_row)])

    def swap_pair(value):
        return lax.ppermute(value, "col", [(i, i ^ 1) for i in range(n_col)])

    def line_all_to_all(value):
        return lax.all_to_all(value, "col", 0, 0, axis_index_groups=lines, tiled=True)

    near, first = pl.pallas_call(
        panel_kernel,
        out_shape=(shape((nodes, feats), bf), token),
        in_specs=[HBM] * 3,
        out_specs=(VMEM, VMEM),
        scratch_shapes=[
            pltpu.VMEM((nodes, width), bf),
            pltpu.VMEM((nodes, width), jnp.int32),
            pltpu.VMEM((feats, width), bf),
            pltpu.SemaphoreType.DMA((3,)),
        ],
        compiler_params=params(53.75),
        cost_estimate=cost(2 * nodes * width * feats, nodes * width * 8),
    )(grad_out, relu_mask, weight)

    four = swap(near, 4)

    term, ready = pl.pallas_call(
        weight_kernel,
        out_shape=(shape((width // LANES * feats, LANES), bf), token),
        in_specs=[HBM] * 3 + [VMEM],
        out_specs=(VMEM, VMEM),
        scratch_shapes=[
            pltpu.VMEM((nodes, width), bf),
            pltpu.VMEM((nodes, width), jnp.int32),
            pltpu.VMEM((nodes, feats), bf),
            pltpu.SemaphoreType.DMA((3,)),
        ],
        compiler_params=params(53.9),
        cost_estimate=cost(2 * 10**10, nodes * width * 4),
    )(grad_out, relu_mask, aggregated, first)
    spread = line_all_to_all(term.reshape(n_y, term.shape[0] // n_y, LANES))
    extra = spread.shape[1]
    packed = pl.pallas_call(
        pack_kernel,
        out_shape=shape((2 * nodes, feats), bf),
        in_specs=[VMEM] * 3,
        out_specs=VMEM,
        compiler_params=params(16),
        cost_estimate=cost(2 * 10**10, nodes * feats * 8),
    )(ready, near, four)
    got_1, got_2, got_3 = swap(packed, 1), swap(packed, 2), swap(packed, 3)

    share = pl.pallas_call(
        sum_kernel,
        out_shape=shape((extra, LANES), bf),
        in_specs=[HBM, VMEM],
        out_specs=VMEM,
        compiler_params=params(16),
        cost_estimate=cost(2 * 10**10, n_y * extra * LANES * 2),
    )(packed, spread)
    row_1 = swap(share, 1)

    live = tile_count[0, 0]
    away = (tile_col[0, 0] * size // nodes) ^ lax.axis_index("row")
    chunk = (away & 3) * 2 + (away >> 2)
    col_at = chunk * per_owner + tile_col[0, 0] % per_owner
    room = -(-(slots + block_tiles) // (2 * GROUP)) * GROUP
    pairs, order, cols, rows = pl.pallas_call(
        functools.partial(prepare_kernel, n_row * per_owner),
        out_shape=(
            shape((1,), jnp.int32),
            shape((2 * room,), jnp.int32),
            shape((2 * room,), jnp.int32),
            shape((room,), jnp.int32),
        ),
        in_specs=[SMEM] * 3 + [HBM],
        out_specs=(SMEM,) * 4,
        scratch_shapes=[
            pltpu.SMEM((block_tiles,), jnp.int32),
            pltpu.SMEM((block_tiles,), jnp.int32),
        ],
        compiler_params=params(16),
        cost_estimate=cost(2 * 10**10, slots * 8),
    )(live.reshape(1), tile_row[0, 0], col_at, packed)

    sent = pl.pallas_call(
        tiles_kernel,
        out_shape=shape((n_y, PAIR * nodes, feats), bf),
        in_specs=[SMEM] * 5 + [HBM] + [VMEM] * 5,
        out_specs=HBM,
        scratch_shapes=[
            pltpu.VMEM((slots, size, size), bf),
            pltpu.VMEM((n_row * per_owner + 1, size, feats), bf),
            pltpu.VMEM((block_tiles + 1, size, feats), f32),
            pltpu.VMEM((n_y, PAIR * nodes, feats), bf),
            pltpu.SemaphoreType.DMA((slots // CHUNK,)),
            pltpu.SemaphoreType.DMA((n_y,)),
        ],
        compiler_params=params(50),
        cost_estimate=cost(2 * 10**10, slots * size * size * 2),
    )(live.reshape(1), pairs, order, cols, rows, tile_data, near, four, got_1, got_2, got_3)
    sent, share = pl.pallas_call(
        pair_kernel,
        out_shape=(shape(sent.shape, bf), shape((extra, LANES), bf)),
        in_specs=[HBM] + [VMEM] * 2,
        out_specs=(HBM, VMEM),
        input_output_aliases={0: 0},
        compiler_params=params(16),
        cost_estimate=cost(4 * extra * LANES, 4 * extra * LANES * 2),
    )(sent, share, row_1)
    got = line_all_to_all(sent)
    for mask in (2, 4):
        share = (share.astype(f32) + swap(share, mask).astype(f32)).astype(bf)
    far = swap_pair(share)

    half = (lax.axis_index("col") & (PAIR - 1)).astype(jnp.int32).reshape(1)
    keep, send = pl.pallas_call(
        halves_kernel,
        out_shape=(shape((nodes, feats), f32), shape((nodes, feats), bf)),
        in_specs=[SMEM, VMEM],
        out_specs=(VMEM, VMEM),
        scratch_shapes=[pltpu.VMEM((PAIR * nodes, feats), f32)],
        compiler_params=params(16),
        cost_estimate=cost(nodes * feats * n_col, nodes * feats * n_col * 2),
    )(half, got)
    other = swap_pair(send)
    whole = pl.pallas_call(
        share_kernel,
        out_shape=shape((n_y, extra, LANES), bf),
        in_specs=[HBM] + [VMEM] * 2,
        out_specs=VMEM,
        compiler_params=params(16),
        cost_estimate=cost(2 * 10**10, n_y * extra * LANES * 2),
    )(send, share, far)
    shares = line_all_to_all(whole)
    features, after = pl.pallas_call(
        features_kernel,
        out_shape=(shape((nodes, feats), bf), token),
        in_specs=[VMEM] * 2,
        out_specs=(VMEM, VMEM),
        compiler_params=params(16),
        cost_estimate=cost(2 * 10**10, nodes * feats * 4),
    )(keep, other)
    grad_weight = pl.pallas_call(
        spread_kernel,
        out_shape=shape((feats, width), f32),
        in_specs=[HBM, VMEM],
        out_specs=VMEM,
        compiler_params=params(16),
        cost_estimate=cost(feats * width, feats * width * 6),
    )(after, shares)
    return features, grad_weight


def solution(mesh):
    placed = (
        P(("col", "row"), None),
        P(("col", "row"), None),
        P(("col", "row"), "depth"),
        P("depth", None),
        P("row", "col", None, None, None),
        P("row", "col", None),
        P("row", "col", None),
        P("row", "col"),
    )
    return jax.shard_map(
        shards,
        mesh=mesh,
        in_specs=placed,
        out_specs=(P(("row", "col"), "depth"), P("depth", None)),
        check_vma=False,
    )
```

```python
import jax
import jax.numpy as jnp
from jax import lax
from jax.experimental import pallas as pl
from jax.experimental.pallas import tpu as pltpu
from jax.sharding import PartitionSpec as P

LANES = 128
GROUP = 32
PAIR = 2
VMEM = pl.BlockSpec(memory_space=pltpu.VMEM)
SMEM = pl.BlockSpec(memory_space=pltpu.SMEM)
HBM = pl.BlockSpec(memory_space=pl.ANY)


def params(mib):
    return pltpu.CompilerParams(vmem_limit_bytes=int(mib * 2**20))


def cost(flops, moved):
    return pl.CostEstimate(flops=flops, bytes_accessed=moved, transcendentals=0)


def panel_kernel(
    grad_hbm, mask_hbm, weight_hbm, panel_ref, after_ref, grad, mask, weight, arrived
):
    after_ref[...] = jnp.zeros_like(after_ref)
    copies = [
        pltpu.make_async_copy(mask_hbm, mask, arrived.at[0]),
        pltpu.make_async_copy(grad_hbm, grad, arrived.at[1]),
        pltpu.make_async_copy(weight_hbm, weight, arrived.at[2]),
    ]
    for copy in copies:
        copy.start()
    for copy in copies:
        copy.wait()
    masked = grad[...] * mask[...].astype(jnp.float32).astype(jnp.bfloat16)
    panel_ref[...] = lax.dot_general(
        masked, weight[...], (((1,), (1,)), ((), ())), preferred_element_type=jnp.float32
    ).astype(jnp.bfloat16)


def weight_kernel(
    grad_hbm, mask_hbm, aggregated_hbm, before_ref, out_ref, after_ref, grad, mask, aggregated, arrived
):
    copies = [
        pltpu.make_async_copy(mask_hbm, mask, arrived.at[0]),
        pltpu.make_async_copy(grad_hbm, grad, arrived.at[1]),
        pltpu.make_async_copy(aggregated_hbm, aggregated, arrived.at[2]),
    ]
    for copy in copies:
        copy.start()
    for copy in copies:
        copy.wait()
    after_ref[...] = jnp.zeros_like(after_ref)
    flipped = aggregated[...].T
    feats = flipped.shape[0]
    for j in range(grad.shape[1] // LANES):
        part = slice(j * LANES, (j + 1) * LANES)
        masked = grad[:, part] * mask[:, part].astype(jnp.float32).astype(jnp.bfloat16)
        term = jnp.dot(flipped, masked, preferred_element_type=jnp.float32)
        out_ref[j * feats : (j + 1) * feats, :] = term.astype(jnp.bfloat16)


def pack_kernel(after_ref, near, four, packed_ref):
    nodes = near.shape[0]
    packed_ref[0:nodes, :] = near[...]
    packed_ref[nodes : 2 * nodes, :] = four[...]


def sum_kernel(after_ref, spread_ref, out_ref):
    acc = spread_ref[0].astype(jnp.float32)
    for c in range(1, spread_ref.shape[0]):
        acc = acc + spread_ref[c].astype(jnp.float32)
    out_ref[...] = acc.astype(jnp.bfloat16)


def pair_kernel(sent_in, own, other, sent_out, out_ref):
    total = own[...].astype(jnp.float32) + other[...].astype(jnp.float32)
    out_ref[...] = total.astype(jnp.bfloat16)


def tiles_kernel(
    live_ref, row_ref, col_ref, tiles_hbm, near, four, got_1, got_2, got_3, out_hbm,
    tiles, panel, total, done, arrived, written,
):
    size = tiles.shape[1]
    groups = (live_ref[0] + GROUP - 1) // GROUP

    def fetch(g):
        part = pl.ds(g * GROUP, GROUP)
        return pltpu.make_async_copy(tiles_hbm.at[part], tiles.at[part], arrived.at[g])

    for g in range(tiles.shape[0] // GROUP):
        pl.when(g < groups)(fetch(g).start)
    total[...] = jnp.zeros_like(total)
    place = 0
    for part in (near, four, got_1, got_2, got_3):
        for k in range(part.shape[0] // size):
            panel[place] = part[k * size : (k + 1) * size, :]
            place += 1

    def group(g, carry):
        fetch(g).wait()
        first = g * GROUP
        terms = []
        for u in range(GROUP):
            terms.append(
                jnp.dot(
                    tiles[first + u], panel[col_ref[first + u]], preferred_element_type=jnp.float32
                )
            )
        for u in range(GROUP):
            r = row_ref[first + u]
            total[r] = total[r] + terms[u]
        return carry

    lax.fori_loop(0, groups, group, 0)
    owners, height = done.shape[0], done.shape[1]
    results = []
    for c in range(owners):
        for k in range(height // size):
            done[c, k * size : (k + 1) * size, :] = total[c * (height // size) + k].astype(
                jnp.bfloat16
            )
        results.append(pltpu.make_async_copy(done.at[c], out_hbm.at[c], written.at[c]))
        results[-1].start()
    for result in results:
        result.wait()


def halves_kernel(half_ref, got_ref, keep_ref, send_ref, total):
    owners, height = got_ref.shape[0], got_ref.shape[1]
    for k in range(height // LANES):
        rows = slice(k * LANES, (k + 1) * LANES)
        acc = got_ref[0, rows, :].astype(jnp.float32)
        for c in range(1, owners):
            acc = acc + got_ref[c, rows, :].astype(jnp.float32)
        total[rows, :] = acc
    own = keep_ref.shape[0]
    half = half_ref[0]
    keep_ref[...] = total[pl.ds(pl.multiple_of(half * own, own), own), :]
    send_ref[...] = total[pl.ds(pl.multiple_of((1 - half) * own, own), own), :].astype(jnp.bfloat16)


def share_kernel(after_ref, own, other, out_ref):
    total = own[...].astype(jnp.float32) + other[...].astype(jnp.float32)
    total = total.astype(jnp.bfloat16)
    for c in range(out_ref.shape[0]):
        out_ref[c] = total


def features_kernel(keep_ref, got_ref, features_ref, after_ref):
    after_ref[...] = jnp.zeros_like(after_ref)
    features_ref[...] = (keep_ref[...] + got_ref[...].astype(jnp.float32)).astype(jnp.bfloat16)


def spread_kernel(after_ref, shares_ref, weight_ref):
    owners, rows = shares_ref.shape[0], shares_ref.shape[1]
    feats = weight_ref.shape[0]
    for g in range(owners * rows // feats):
        c, at = g * feats // rows, g * feats % rows
        weight_ref[:, g * LANES : (g + 1) * LANES] = shares_ref[c, at : at + feats, :].astype(
            jnp.float32
        )


def shards(grad_out, relu_mask, aggregated, weight, adj_tiles, tile_row, tile_col, tile_count):
    n_row, n_col = lax.axis_size("row"), lax.axis_size("col")
    n_y = n_col // PAIR
    lines = [[y * PAIR + h for y in range(n_y)] for h in range(PAIR)]
    nodes, width = grad_out.shape
    feats = weight.shape[0]
    tile_data = adj_tiles[0, 0]
    slots, size = tile_data.shape[0], tile_data.shape[1]
    block_tiles = nodes * n_col // size
    per_owner = nodes // size
    bf, f32 = jnp.bfloat16, jnp.float32
    shape = jax.ShapeDtypeStruct
    token = shape((8, LANES), f32)

    def swap(value, mask):
        return lax.ppermute(value, "row", [(i, i ^ mask) for i in range(n_row)])

    def swap_pair(value):
        return lax.ppermute(value, "col", [(i, i ^ 1) for i in range(n_col)])

    def line_all_to_all(value):
        return lax.all_to_all(value, "col", 0, 0, axis_index_groups=lines, tiled=True)

    near, first = pl.pallas_call(
        panel_kernel,
        out_shape=(shape((nodes, feats), bf), token),
        in_specs=[HBM] * 3,
        out_specs=(VMEM, VMEM),
        scratch_shapes=[
            pltpu.VMEM((nodes, width), bf),
            pltpu.VMEM((nodes, width), jnp.int32),
            pltpu.VMEM((feats, width), bf),
            pltpu.SemaphoreType.DMA((3,)),
        ],
        compiler_params=params(53.75),
        cost_estimate=cost(2 * nodes * width * feats, nodes * width * 8),
    )(grad_out, relu_mask, weight)

    four = swap(near, 4)

    term, ready = pl.pallas_call(
        weight_kernel,
        out_shape=(shape((width // LANES * feats, LANES), bf), token),
        in_specs=[HBM] * 3 + [VMEM],
        out_specs=(VMEM, VMEM),
        scratch_shapes=[
            pltpu.VMEM((nodes, width), bf),
            pltpu.VMEM((nodes, width), jnp.int32),
            pltpu.VMEM((nodes, feats), bf),
            pltpu.SemaphoreType.DMA((3,)),
        ],
        compiler_params=params(53.9),
        cost_estimate=cost(2 * 10**10, nodes * width * 4),
    )(grad_out, relu_mask, aggregated, first)
    spread = line_all_to_all(term.reshape(n_y, term.shape[0] // n_y, LANES))
    extra = spread.shape[1]
    packed = pl.pallas_call(
        pack_kernel,
        out_shape=shape((2 * nodes, feats), bf),
        in_specs=[VMEM] * 3,
        out_specs=VMEM,
        compiler_params=params(16),
        cost_estimate=cost(2 * 10**10, nodes * feats * 8),
    )(ready, near, four)
    got_1, got_2, got_3 = swap(packed, 1), swap(packed, 2), swap(packed, 3)

    share = pl.pallas_call(
        sum_kernel,
        out_shape=shape((extra, LANES), bf),
        in_specs=[HBM, VMEM],
        out_specs=VMEM,
        compiler_params=params(16),
        cost_estimate=cost(2 * 10**10, n_y * extra * LANES * 2),
    )(packed, spread)
    row_1 = swap(share, 1)

    live = tile_count[0, 0]
    away = (tile_col[0, 0] * size // nodes) ^ lax.axis_index("row")
    chunk = (away & 3) * 2 + (away >> 2)
    col_at = chunk * per_owner + tile_col[0, 0] % per_owner
    row_at = jnp.where(jnp.arange(slots, dtype=jnp.int32) < live, tile_row[0, 0], block_tiles)

    sent = pl.pallas_call(
        tiles_kernel,
        out_shape=shape((n_y, PAIR * nodes, feats), bf),
        in_specs=[SMEM] * 3 + [HBM] + [VMEM] * 5,
        out_specs=HBM,
        scratch_shapes=[
            pltpu.VMEM((slots, size, size), bf),
            pltpu.VMEM((n_row * per_owner, size, feats), bf),
            pltpu.VMEM((block_tiles + 1, size, feats), f32),
            pltpu.VMEM((n_y, PAIR * nodes, feats), bf),
            pltpu.SemaphoreType.DMA((slots // GROUP,)),
            pltpu.SemaphoreType.DMA((n_y,)),
        ],
        compiler_params=params(50),
        cost_estimate=cost(2 * 10**10, slots * size * size * 2),
    )(live.reshape(1), row_at, col_at, tile_data, near, four, got_1, got_2, got_3)
    sent, share = pl.pallas_call(
        pair_kernel,
        out_shape=(shape(sent.shape, bf), shape((extra, LANES), bf)),
        in_specs=[HBM] + [VMEM] * 2,
        out_specs=(HBM, VMEM),
        input_output_aliases={0: 0},
        compiler_params=params(16),
        cost_estimate=cost(4 * extra * LANES, 4 * extra * LANES * 2),
    )(sent, share, row_1)
    got = line_all_to_all(sent)
    for mask in (2, 4):
        share = (share.astype(f32) + swap(share, mask).astype(f32)).astype(bf)
    far = swap_pair(share)

    half = (lax.axis_index("col") & (PAIR - 1)).astype(jnp.int32).reshape(1)
    keep, send = pl.pallas_call(
        halves_kernel,
        out_shape=(shape((nodes, feats), f32), shape((nodes, feats), bf)),
        in_specs=[SMEM, VMEM],
        out_specs=(VMEM, VMEM),
        scratch_shapes=[pltpu.VMEM((PAIR * nodes, feats), f32)],
        compiler_params=params(16),
        cost_estimate=cost(nodes * feats * n_col, nodes * feats * n_col * 2),
    )(half, got)
    other = swap_pair(send)
    whole = pl.pallas_call(
        share_kernel,
        out_shape=shape((n_y, extra, LANES), bf),
        in_specs=[HBM] + [VMEM] * 2,
        out_specs=VMEM,
        compiler_params=params(16),
        cost_estimate=cost(2 * 10**10, n_y * extra * LANES * 2),
    )(send, share, far)
    shares = line_all_to_all(whole)
    features, after = pl.pallas_call(
        features_kernel,
        out_shape=(shape((nodes, feats), bf), token),
        in_specs=[VMEM] * 2,
        out_specs=(VMEM, VMEM),
        compiler_params=params(16),
        cost_estimate=cost(2 * 10**10, nodes * feats * 4),
    )(keep, other)
    grad_weight = pl.pallas_call(
        spread_kernel,
        out_shape=shape((feats, width), f32),
        in_specs=[HBM, VMEM],
        out_specs=VMEM,
        compiler_params=params(16),
        cost_estimate=cost(feats * width, feats * width * 6),
    )(after, shares)
    return features, grad_weight


def solution(mesh):
    placed = (
        P(("col", "row"), None),
        P(("col", "row"), None),
        P(("col", "row"), "depth"),
        P("depth", None),
        P("row", "col", None, None, None),
        P("row", "col", None),
        P("row", "col", None),
        P("row", "col"),
    )
    return jax.shard_map(
        shards,
        mesh=mesh,
        in_specs=placed,
        out_specs=(P(("row", "col"), "depth"), P("depth", None)),
        check_vma=False,
    )
```

```python
import jax
import jax.numpy as jnp
from jax import lax
from jax.experimental import pallas as pl
from jax.experimental.pallas import tpu as pltpu
from jax.sharding import PartitionSpec as P

LANES = 128
GROUP = 32
PAIR = 2
VMEM = pl.BlockSpec(memory_space=pltpu.VMEM)
SMEM = pl.BlockSpec(memory_space=pltpu.SMEM)
HBM = pl.BlockSpec(memory_space=pl.ANY)


def params(mib):
    return pltpu.CompilerParams(vmem_limit_bytes=int(mib * 2**20))


def cost(flops, moved):
    return pl.CostEstimate(flops=flops, bytes_accessed=moved, transcendentals=0)


def panel_kernel(
    grad_hbm, mask_hbm, weight_hbm, panel_ref, after_ref, grad, mask, weight, arrived
):
    after_ref[...] = jnp.zeros_like(after_ref)
    copies = [
        pltpu.make_async_copy(mask_hbm, mask, arrived.at[0]),
        pltpu.make_async_copy(grad_hbm, grad, arrived.at[1]),
        pltpu.make_async_copy(weight_hbm, weight, arrived.at[2]),
    ]
    for copy in copies:
        copy.start()
    for copy in copies:
        copy.wait()
    masked = grad[...] * mask[...].astype(jnp.float32).astype(jnp.bfloat16)
    panel_ref[...] = lax.dot_general(
        masked, weight[...], (((1,), (1,)), ((), ())), preferred_element_type=jnp.float32
    ).astype(jnp.bfloat16)


def weight_kernel(
    grad_hbm, mask_hbm, aggregated_hbm, before_ref, out_ref, after_ref, grad, mask, aggregated, arrived
):
    copies = [
        pltpu.make_async_copy(mask_hbm, mask, arrived.at[0]),
        pltpu.make_async_copy(grad_hbm, grad, arrived.at[1]),
        pltpu.make_async_copy(aggregated_hbm, aggregated, arrived.at[2]),
    ]
    for copy in copies:
        copy.start()
    for copy in copies:
        copy.wait()
    after_ref[...] = jnp.zeros_like(after_ref)
    flipped = aggregated[...].T
    feats = flipped.shape[0]
    for j in range(grad.shape[1] // LANES):
        part = slice(j * LANES, (j + 1) * LANES)
        masked = grad[:, part] * mask[:, part].astype(jnp.float32).astype(jnp.bfloat16)
        term = jnp.dot(flipped, masked, preferred_element_type=jnp.float32)
        out_ref[j * feats : (j + 1) * feats, :] = term.astype(jnp.bfloat16)


def pack_kernel(after_ref, near, four, packed_ref):
    nodes = near.shape[0]
    packed_ref[0:nodes, :] = near[...]
    packed_ref[nodes : 2 * nodes, :] = four[...]


def sum_kernel(after_ref, spread_ref, out_ref):
    acc = spread_ref[0].astype(jnp.float32)
    for c in range(1, spread_ref.shape[0]):
        acc = acc + spread_ref[c].astype(jnp.float32)
    out_ref[...] = acc.astype(jnp.bfloat16)


def pair_kernel(sent_in, own, other, sent_out, out_ref):
    total = own[...].astype(jnp.float32) + other[...].astype(jnp.float32)
    out_ref[...] = total.astype(jnp.bfloat16)


def tiles_kernel(
    live_ref, row_ref, col_ref, tiles_hbm, near, four, got_1, got_2, got_3, out_hbm,
    tiles, panel, total, done, arrived, written,
):
    size = tiles.shape[1]
    groups = (live_ref[0] + GROUP - 1) // GROUP

    def fetch(g):
        part = pl.ds(g * GROUP, GROUP)
        return pltpu.make_async_copy(tiles_hbm.at[part], tiles.at[part], arrived.at[g])

    for g in range(tiles.shape[0] // GROUP):
        pl.when(g < groups)(fetch(g).start)
    total[...] = jnp.zeros_like(total)
    place = 0
    for part in (near, four, got_1, got_2, got_3):
        for k in range(part.shape[0] // size):
            panel[place] = part[k * size : (k + 1) * size, :]
            place += 1

    def group(g, carry):
        fetch(g).wait()
        first = g * GROUP
        terms = []
        for u in range(GROUP):
            terms.append(
                jnp.dot(
                    tiles[first + u], panel[col_ref[first + u]], preferred_element_type=jnp.float32
                )
            )
        for u in range(GROUP):
            r = row_ref[first + u]
            total[r] = total[r] + terms[u]
        return carry

    lax.fori_loop(0, groups, group, 0)
    owners, height = done.shape[0], done.shape[1]
    results = []
    for c in range(owners):
        for k in range(height // size):
            done[c, k * size : (k + 1) * size, :] = total[c * (height // size) + k].astype(
                jnp.bfloat16
            )
        results.append(pltpu.make_async_copy(done.at[c], out_hbm.at[c], written.at[c]))
        results[-1].start()
    for result in results:
        result.wait()


def halves_kernel(half_ref, got_ref, keep_ref, send_ref, total):
    owners, height = got_ref.shape[0], got_ref.shape[1]
    for k in range(height // LANES):
        rows = slice(k * LANES, (k + 1) * LANES)
        acc = got_ref[0, rows, :].astype(jnp.float32)
        for c in range(1, owners):
            acc = acc + got_ref[c, rows, :].astype(jnp.float32)
        total[rows, :] = acc
    own = keep_ref.shape[0]
    half = half_ref[0]
    keep_ref[...] = total[pl.ds(pl.multiple_of(half * own, own), own), :]
    send_ref[...] = total[pl.ds(pl.multiple_of((1 - half) * own, own), own), :].astype(jnp.bfloat16)


def share_kernel(after_ref, own, other, out_ref):
    total = own[...].astype(jnp.float32) + other[...].astype(jnp.float32)
    total = total.astype(jnp.bfloat16)
    for c in range(out_ref.shape[0]):
        out_ref[c] = total


def features_kernel(keep_ref, got_ref, features_ref, after_ref):
    after_ref[...] = jnp.zeros_like(after_ref)
    features_ref[...] = (keep_ref[...] + got_ref[...].astype(jnp.float32)).astype(jnp.bfloat16)


def spread_kernel(after_ref, shares_ref, weight_ref):
    owners, rows = shares_ref.shape[0], shares_ref.shape[1]
    feats = weight_ref.shape[0]
    for g in range(owners * rows // feats):
        c, at = g * feats // rows, g * feats % rows
        weight_ref[:, g * LANES : (g + 1) * LANES] = shares_ref[c, at : at + feats, :].astype(
            jnp.float32
        )


def shards(grad_out, relu_mask, aggregated, weight, adj_tiles, tile_row, tile_col, tile_count):
    n_row, n_col = lax.axis_size("row"), lax.axis_size("col")
    n_y = n_col // PAIR
    lines = [[y * PAIR + h for y in range(n_y)] for h in range(PAIR)]
    nodes, width = grad_out.shape
    feats = weight.shape[0]
    tile_data = adj_tiles[0, 0]
    slots, size = tile_data.shape[0], tile_data.shape[1]
    block_tiles = nodes * n_col // size
    per_owner = nodes // size
    bf, f32 = jnp.bfloat16, jnp.float32
    shape = jax.ShapeDtypeStruct
    token = shape((8, LANES), f32)

    def swap(value, mask):
        return lax.ppermute(value, "row", [(i, i ^ mask) for i in range(n_row)])

    def swap_pair(value):
        return lax.ppermute(value, "col", [(i, i ^ 1) for i in range(n_col)])

    def line_all_to_all(value):
        return lax.all_to_all(value, "col", 0, 0, axis_index_groups=lines, tiled=True)

    near, first = pl.pallas_call(
        panel_kernel,
        out_shape=(shape((nodes, feats), bf), token),
        in_specs=[HBM] * 3,
        out_specs=(VMEM, VMEM),
        scratch_shapes=[
            pltpu.VMEM((nodes, width), bf),
            pltpu.VMEM((nodes, width), jnp.int32),
            pltpu.VMEM((feats, width), bf),
            pltpu.SemaphoreType.DMA((3,)),
        ],
        compiler_params=params(53.75),
        cost_estimate=cost(2 * nodes * width * feats, nodes * width * 8),
    )(grad_out, relu_mask, weight)

    four = swap(near, 4)

    term, ready = pl.pallas_call(
        weight_kernel,
        out_shape=(shape((width // LANES * feats, LANES), bf), token),
        in_specs=[HBM] * 3 + [VMEM],
        out_specs=(VMEM, VMEM),
        scratch_shapes=[
            pltpu.VMEM((nodes, width), bf),
            pltpu.VMEM((nodes, width), jnp.int32),
            pltpu.VMEM((nodes, feats), bf),
            pltpu.SemaphoreType.DMA((3,)),
        ],
        compiler_params=params(53.9),
        cost_estimate=cost(2 * 10**10, nodes * width * 4),
    )(grad_out, relu_mask, aggregated, first)
    spread = line_all_to_all(term.reshape(n_y, term.shape[0] // n_y, LANES))
    extra = spread.shape[1]
    packed = pl.pallas_call(
        pack_kernel,
        out_shape=shape((2 * nodes, feats), bf),
        in_specs=[VMEM] * 3,
        out_specs=VMEM,
        compiler_params=params(16),
        cost_estimate=cost(2 * 10**10, nodes * feats * 8),
    )(ready, near, four)
    got_1, got_2, got_3 = swap(packed, 1), swap(packed, 2), swap(packed, 3)

    share = pl.pallas_call(
        sum_kernel,
        out_shape=shape((extra, LANES), bf),
        in_specs=[HBM, VMEM],
        out_specs=VMEM,
        compiler_params=params(16),
        cost_estimate=cost(2 * 10**10, n_y * extra * LANES * 2),
    )(packed, spread)
    row_1 = swap(share, 1)

    live = tile_count[0, 0]
    away = (tile_col[0, 0] * size // nodes) ^ lax.axis_index("row")
    chunk = (away & 3) * 2 + (away >> 2)
    col_at = chunk * per_owner + tile_col[0, 0] % per_owner
    row_at = jnp.where(jnp.arange(slots, dtype=jnp.int32) < live, tile_row[0, 0], block_tiles)

    sent = pl.pallas_call(
        tiles_kernel,
        out_shape=shape((n_y, PAIR * nodes, feats), bf),
        in_specs=[SMEM] * 3 + [HBM] + [VMEM] * 5,
        out_specs=HBM,
        scratch_shapes=[
            pltpu.VMEM((slots, size, size), bf),
            pltpu.VMEM((n_row * per_owner, size, feats), bf),
            pltpu.VMEM((block_tiles + 1, size, feats), f32),
            pltpu.VMEM((n_y, PAIR * nodes, feats), bf),
            pltpu.SemaphoreType.DMA((slots // GROUP,)),
            pltpu.SemaphoreType.DMA((n_y,)),
        ],
        compiler_params=params(50),
        cost_estimate=cost(2 * 10**10, slots * size * size * 2),
    )(live.reshape(1), row_at, col_at, tile_data, near, four, got_1, got_2, got_3)
    sent, share = pl.pallas_call(
        pair_kernel,
        out_shape=(shape(sent.shape, bf), shape((extra, LANES), bf)),
        in_specs=[HBM] + [VMEM] * 2,
        out_specs=(HBM, VMEM),
        input_output_aliases={0: 0},
        compiler_params=params(16),
        cost_estimate=cost(4 * extra * LANES, 4 * extra * LANES * 2),
    )(sent, share, row_1)
    got = line_all_to_all(sent)
    share = (share.astype(f32) + swap_pair(share).astype(f32)).astype(bf)
    share = (share.astype(f32) + swap(share, 2).astype(f32)).astype(bf)
    far = swap(share, 4)

    half = (lax.axis_index("col") & (PAIR - 1)).astype(jnp.int32).reshape(1)
    keep, send = pl.pallas_call(
        halves_kernel,
        out_shape=(shape((nodes, feats), f32), shape((nodes, feats), bf)),
        in_specs=[SMEM, VMEM],
        out_specs=(VMEM, VMEM),
        scratch_shapes=[pltpu.VMEM((PAIR * nodes, feats), f32)],
        compiler_params=params(16),
        cost_estimate=cost(nodes * feats * n_col, nodes * feats * n_col * 2),
    )(half, got)
    other = swap_pair(send)
    whole = pl.pallas_call(
        share_kernel,
        out_shape=shape((n_y, extra, LANES), bf),
        in_specs=[HBM] + [VMEM] * 2,
        out_specs=VMEM,
        compiler_params=params(16),
        cost_estimate=cost(2 * 10**10, n_y * extra * LANES * 2),
    )(send, share, far)
    shares = line_all_to_all(whole)
    features, after = pl.pallas_call(
        features_kernel,
        out_shape=(shape((nodes, feats), bf), token),
        in_specs=[VMEM] * 2,
        out_specs=(VMEM, VMEM),
        compiler_params=params(16),
        cost_estimate=cost(2 * 10**10, nodes * feats * 4),
    )(keep, other)
    grad_weight = pl.pallas_call(
        spread_kernel,
        out_shape=shape((feats, width), f32),
        in_specs=[HBM, VMEM],
        out_specs=VMEM,
        compiler_params=params(16),
        cost_estimate=cost(feats * width, feats * width * 6),
    )(after, shares)
    return features, grad_weight


def solution(mesh):
    placed = (
        P(("col", "row"), None),
        P(("col", "row"), None),
        P(("col", "row"), "depth"),
        P("depth", None),
        P("row", "col", None, None, None),
        P("row", "col", None),
        P("row", "col", None),
        P("row", "col"),
    )
    return jax.shard_map(
        shards,
        mesh=mesh,
        in_specs=placed,
        out_specs=(P(("row", "col"), "depth"), P("depth", None)),
        check_vma=False,
    )
```

```python
import jax
import jax.numpy as jnp
from jax import lax
from jax.experimental import pallas as pl
from jax.experimental.pallas import tpu as pltpu
from jax.sharding import PartitionSpec as P

LANES = 128
GROUP = 32
PAIR = 2
VMEM = pl.BlockSpec(memory_space=pltpu.VMEM)
SMEM = pl.BlockSpec(memory_space=pltpu.SMEM)
HBM = pl.BlockSpec(memory_space=pl.ANY)


def params(mib):
    return pltpu.CompilerParams(vmem_limit_bytes=int(mib * 2**20))


def cost(flops, moved):
    return pl.CostEstimate(flops=flops, bytes_accessed=moved, transcendentals=0)


def panel_kernel(
    grad_hbm, mask_hbm, weight_hbm, panel_ref, after_ref, grad, mask, weight, arrived
):
    after_ref[...] = jnp.zeros_like(after_ref)
    copies = [
        pltpu.make_async_copy(mask_hbm, mask, arrived.at[0]),
        pltpu.make_async_copy(grad_hbm, grad, arrived.at[1]),
        pltpu.make_async_copy(weight_hbm, weight, arrived.at[2]),
    ]
    for copy in copies:
        copy.start()
    for copy in copies:
        copy.wait()
    masked = grad[...] * mask[...].astype(jnp.float32).astype(jnp.bfloat16)
    panel_ref[...] = lax.dot_general(
        masked, weight[...], (((1,), (1,)), ((), ())), preferred_element_type=jnp.float32
    ).astype(jnp.bfloat16)


def weight_kernel(
    grad_hbm, mask_hbm, aggregated_hbm, before_ref, out_ref, after_ref, grad, mask, aggregated, arrived
):
    copies = [
        pltpu.make_async_copy(mask_hbm, mask, arrived.at[0]),
        pltpu.make_async_copy(grad_hbm, grad, arrived.at[1]),
        pltpu.make_async_copy(aggregated_hbm, aggregated, arrived.at[2]),
    ]
    for copy in copies:
        copy.start()
    for copy in copies:
        copy.wait()
    after_ref[...] = jnp.zeros_like(after_ref)
    flipped = aggregated[...].T
    feats = flipped.shape[0]
    for j in range(grad.shape[1] // LANES):
        part = slice(j * LANES, (j + 1) * LANES)
        masked = grad[:, part] * mask[:, part].astype(jnp.float32).astype(jnp.bfloat16)
        term = jnp.dot(flipped, masked, preferred_element_type=jnp.float32)
        out_ref[j * feats : (j + 1) * feats, :] = term.astype(jnp.bfloat16)


def pack_kernel(after_ref, near, four, packed_ref):
    nodes = near.shape[0]
    packed_ref[0:nodes, :] = near[...]
    packed_ref[nodes : 2 * nodes, :] = four[...]


def sum_kernel(after_ref, spread_ref, out_ref):
    acc = spread_ref[0].astype(jnp.float32)
    for c in range(1, spread_ref.shape[0]):
        acc = acc + spread_ref[c].astype(jnp.float32)
    out_ref[...] = acc.astype(jnp.bfloat16)


def pair_kernel(sent_in, own, other, sent_out, out_ref):
    total = own[...].astype(jnp.float32) + other[...].astype(jnp.float32)
    out_ref[...] = total.astype(jnp.bfloat16)


def tiles_kernel(
    live_ref, row_ref, col_ref, tiles_hbm, near, four, got_1, got_2, got_3, out_hbm,
    tiles, panel, total, done, arrived, written,
):
    size = tiles.shape[1]
    groups = (live_ref[0] + GROUP - 1) // GROUP

    def fetch(g):
        part = pl.ds(g * GROUP, GROUP)
        return pltpu.make_async_copy(tiles_hbm.at[part], tiles.at[part], arrived.at[g])

    for g in range(tiles.shape[0] // GROUP):
        pl.when(g < groups)(fetch(g).start)
    total[...] = jnp.zeros_like(total)
    place = 0
    for part in (near, four, got_1, got_2, got_3):
        for k in range(part.shape[0] // size):
            panel[place] = part[k * size : (k + 1) * size, :]
            place += 1

    def group(g, carry):
        fetch(g).wait()
        first = g * GROUP
        terms = []
        for u in range(GROUP):
            terms.append(
                jnp.dot(
                    tiles[first + u], panel[col_ref[first + u]], preferred_element_type=jnp.float32
                )
            )
        for u in range(GROUP):
            r = row_ref[first + u]
            total[r] = total[r] + terms[u]
        return carry

    lax.fori_loop(0, groups, group, 0)
    owners, height = done.shape[0], done.shape[1]
    results = []
    for c in range(owners):
        for k in range(height // size):
            done[c, k * size : (k + 1) * size, :] = total[c * (height // size) + k].astype(
                jnp.bfloat16
            )
        results.append(pltpu.make_async_copy(done.at[c], out_hbm.at[c], written.at[c]))
        results[-1].start()
    for result in results:
        result.wait()


def halves_kernel(half_ref, after_ref, got_ref, keep_ref, send_ref, total):
    owners, height = got_ref.shape[0], got_ref.shape[1]
    for k in range(height // LANES):
        rows = slice(k * LANES, (k + 1) * LANES)
        acc = got_ref[0, rows, :].astype(jnp.float32)
        for c in range(1, owners):
            acc = acc + got_ref[c, rows, :].astype(jnp.float32)
        total[rows, :] = acc
    own = keep_ref.shape[0]
    half = half_ref[0]
    keep_ref[...] = total[pl.ds(pl.multiple_of(half * own, own), own), :]
    send_ref[...] = total[pl.ds(pl.multiple_of((1 - half) * own, own), own), :].astype(jnp.bfloat16)


def share_kernel(own, other, out_ref, after_ref):
    after_ref[...] = jnp.zeros_like(after_ref)
    total = own[...].astype(jnp.float32) + other[...].astype(jnp.float32)
    total = total.astype(jnp.bfloat16)
    for c in range(out_ref.shape[0]):
        out_ref[c] = total


def features_kernel(before_ref, keep_ref, got_ref, features_ref):
    features_ref[...] = (keep_ref[...] + got_ref[...].astype(jnp.float32)).astype(jnp.bfloat16)


def spread_kernel(shares_ref, weight_ref, after_ref):
    after_ref[...] = jnp.zeros_like(after_ref)
    owners, rows = shares_ref.shape[0], shares_ref.shape[1]
    feats = weight_ref.shape[0]
    for g in range(owners * rows // feats):
        c, at = g * feats // rows, g * feats % rows
        weight_ref[:, g * LANES : (g + 1) * LANES] = shares_ref[c, at : at + feats, :].astype(
            jnp.float32
        )


def shards(grad_out, relu_mask, aggregated, weight, adj_tiles, tile_row, tile_col, tile_count):
    n_row, n_col = lax.axis_size("row"), lax.axis_size("col")
    n_y = n_col // PAIR
    lines = [[y * PAIR + h for y in range(n_y)] for h in range(PAIR)]
    nodes, width = grad_out.shape
    feats = weight.shape[0]
    tile_data = adj_tiles[0, 0]
    slots, size = tile_data.shape[0], tile_data.shape[1]
    block_tiles = nodes * n_col // size
    per_owner = nodes // size
    bf, f32 = jnp.bfloat16, jnp.float32
    shape = jax.ShapeDtypeStruct
    token = shape((8, LANES), f32)

    def swap(value, mask):
        return lax.ppermute(value, "row", [(i, i ^ mask) for i in range(n_row)])

    def swap_pair(value):
        return lax.ppermute(value, "col", [(i, i ^ 1) for i in range(n_col)])

    def line_all_to_all(value):
        return lax.all_to_all(value, "col", 0, 0, axis_index_groups=lines, tiled=True)

    near, first = pl.pallas_call(
        panel_kernel,
        out_shape=(shape((nodes, feats), bf), token),
        in_specs=[HBM] * 3,
        out_specs=(VMEM, VMEM),
        scratch_shapes=[
            pltpu.VMEM((nodes, width), bf),
            pltpu.VMEM((nodes, width), jnp.int32),
            pltpu.VMEM((feats, width), bf),
            pltpu.SemaphoreType.DMA((3,)),
        ],
        compiler_params=params(53.75),
        cost_estimate=cost(2 * nodes * width * feats, nodes * width * 8),
    )(grad_out, relu_mask, weight)

    four = swap(near, 4)

    term, ready = pl.pallas_call(
        weight_kernel,
        out_shape=(shape((width // LANES * feats, LANES), bf), token),
        in_specs=[HBM] * 3 + [VMEM],
        out_specs=(VMEM, VMEM),
        scratch_shapes=[
            pltpu.VMEM((nodes, width), bf),
            pltpu.VMEM((nodes, width), jnp.int32),
            pltpu.VMEM((nodes, feats), bf),
            pltpu.SemaphoreType.DMA((3,)),
        ],
        compiler_params=params(53.9),
        cost_estimate=cost(2 * 10**10, nodes * width * 4),
    )(grad_out, relu_mask, aggregated, first)
    spread = line_all_to_all(term.reshape(n_y, term.shape[0] // n_y, LANES))
    extra = spread.shape[1]
    packed = pl.pallas_call(
        pack_kernel,
        out_shape=shape((2 * nodes, feats), bf),
        in_specs=[VMEM] * 3,
        out_specs=VMEM,
        compiler_params=params(16),
        cost_estimate=cost(2 * 10**10, nodes * feats * 8),
    )(ready, near, four)
    got_1, got_2, got_3 = swap(packed, 1), swap(packed, 2), swap(packed, 3)

    share = pl.pallas_call(
        sum_kernel,
        out_shape=shape((extra, LANES), bf),
        in_specs=[HBM, VMEM],
        out_specs=VMEM,
        compiler_params=params(16),
        cost_estimate=cost(2 * 10**10, n_y * extra * LANES * 2),
    )(packed, spread)
    row_1 = swap(share, 1)

    live = tile_count[0, 0]
    away = (tile_col[0, 0] * size // nodes) ^ lax.axis_index("row")
    chunk = (away & 3) * 2 + (away >> 2)
    col_at = chunk * per_owner + tile_col[0, 0] % per_owner
    row_at = jnp.where(jnp.arange(slots, dtype=jnp.int32) < live, tile_row[0, 0], block_tiles)

    sent = pl.pallas_call(
        tiles_kernel,
        out_shape=shape((n_y, PAIR * nodes, feats), bf),
        in_specs=[SMEM] * 3 + [HBM] + [VMEM] * 5,
        out_specs=HBM,
        scratch_shapes=[
            pltpu.VMEM((slots, size, size), bf),
            pltpu.VMEM((n_row * per_owner, size, feats), bf),
            pltpu.VMEM((block_tiles + 1, size, feats), f32),
            pltpu.VMEM((n_y, PAIR * nodes, feats), bf),
            pltpu.SemaphoreType.DMA((slots // GROUP,)),
            pltpu.SemaphoreType.DMA((n_y,)),
        ],
        compiler_params=params(50),
        cost_estimate=cost(2 * 10**10, slots * size * size * 2),
    )(live.reshape(1), row_at, col_at, tile_data, near, four, got_1, got_2, got_3)
    sent, share = pl.pallas_call(
        pair_kernel,
        out_shape=(shape(sent.shape, bf), shape((extra, LANES), bf)),
        in_specs=[HBM] + [VMEM] * 2,
        out_specs=(HBM, VMEM),
        input_output_aliases={0: 0},
        compiler_params=params(16),
        cost_estimate=cost(4 * extra * LANES, 4 * extra * LANES * 2),
    )(sent, share, row_1)
    got = line_all_to_all(sent)
    for mask in (2, 4):
        share = (share.astype(f32) + swap(share, mask).astype(f32)).astype(bf)
    far = swap_pair(share)

    whole, ready = pl.pallas_call(
        share_kernel,
        out_shape=(shape((n_y, extra, LANES), bf), token),
        in_specs=[VMEM] * 2,
        out_specs=(VMEM, VMEM),
        compiler_params=params(16),
        cost_estimate=cost(n_y * extra * LANES, n_y * extra * LANES * 2),
    )(share, far)
    shares = line_all_to_all(whole)
    half = (lax.axis_index("col") & (PAIR - 1)).astype(jnp.int32).reshape(1)
    keep, send = pl.pallas_call(
        halves_kernel,
        out_shape=(shape((nodes, feats), f32), shape((nodes, feats), bf)),
        in_specs=[SMEM, HBM, VMEM],
        out_specs=(VMEM, VMEM),
        scratch_shapes=[pltpu.VMEM((PAIR * nodes, feats), f32)],
        compiler_params=params(16),
        cost_estimate=cost(nodes * feats * n_col, nodes * feats * n_col * 2),
    )(half, ready, got)
    other = swap_pair(send)
    grad_weight, after = pl.pallas_call(
        spread_kernel,
        out_shape=(shape((feats, width), f32), token),
        in_specs=[VMEM],
        out_specs=(VMEM, VMEM),
        compiler_params=params(16),
        cost_estimate=cost(feats * width, feats * width * 6),
    )(shares)
    features = pl.pallas_call(
        features_kernel,
        out_shape=shape((nodes, feats), bf),
        in_specs=[HBM] + [VMEM] * 2,
        out_specs=VMEM,
        compiler_params=params(16),
        cost_estimate=cost(nodes * feats, nodes * feats * 4),
    )(after, keep, other)
    return features, grad_weight


def solution(mesh):
    placed = (
        P(("col", "row"), None),
        P(("col", "row"), None),
        P(("col", "row"), "depth"),
        P("depth", None),
        P("row", "col", None, None, None),
        P("row", "col", None),
        P("row", "col", None),
        P("row", "col"),
    )
    return jax.shard_map(
        shards,
        mesh=mesh,
        in_specs=placed,
        out_specs=(P(("row", "col"), "depth"), P("depth", None)),
        check_vma=False,
    )
```

```python
import jax
import jax.numpy as jnp
from jax import lax
from jax.experimental import pallas as pl
from jax.experimental.pallas import tpu as pltpu
from jax.sharding import PartitionSpec as P

LANES = 128
GROUP = 32
PAIR = 2
VMEM = pl.BlockSpec(memory_space=pltpu.VMEM)
SMEM = pl.BlockSpec(memory_space=pltpu.SMEM)
HBM = pl.BlockSpec(memory_space=pl.ANY)


def params(mib):
    return pltpu.CompilerParams(vmem_limit_bytes=int(mib * 2**20))


def cost(flops, moved):
    return pl.CostEstimate(flops=flops, bytes_accessed=moved, transcendentals=0)


def panel_kernel(
    grad_hbm, mask_hbm, weight_hbm, panel_ref, after_ref, grad, mask, weight, arrived
):
    after_ref[...] = jnp.zeros_like(after_ref)
    copies = [
        pltpu.make_async_copy(mask_hbm, mask, arrived.at[0]),
        pltpu.make_async_copy(grad_hbm, grad, arrived.at[1]),
        pltpu.make_async_copy(weight_hbm, weight, arrived.at[2]),
    ]
    for copy in copies:
        copy.start()
    for copy in copies:
        copy.wait()
    masked = grad[...] * mask[...].astype(jnp.float32).astype(jnp.bfloat16)
    panel_ref[...] = lax.dot_general(
        masked, weight[...], (((1,), (1,)), ((), ())), preferred_element_type=jnp.float32
    ).astype(jnp.bfloat16)


def weight_kernel(
    grad_hbm, mask_hbm, aggregated_hbm, before_ref, out_ref, after_ref, grad, mask, aggregated, arrived
):
    copies = [
        pltpu.make_async_copy(mask_hbm, mask, arrived.at[0]),
        pltpu.make_async_copy(grad_hbm, grad, arrived.at[1]),
        pltpu.make_async_copy(aggregated_hbm, aggregated, arrived.at[2]),
    ]
    for copy in copies:
        copy.start()
    for copy in copies:
        copy.wait()
    after_ref[...] = jnp.zeros_like(after_ref)
    flipped = aggregated[...].T
    feats = flipped.shape[0]
    for j in range(grad.shape[1] // LANES):
        part = slice(j * LANES, (j + 1) * LANES)
        masked = grad[:, part] * mask[:, part].astype(jnp.float32).astype(jnp.bfloat16)
        term = jnp.dot(flipped, masked, preferred_element_type=jnp.float32)
        out_ref[j * feats : (j + 1) * feats, :] = term.astype(jnp.bfloat16)


def pack_kernel(after_ref, near, four, packed_ref):
    nodes = near.shape[0]
    packed_ref[0:nodes, :] = near[...]
    packed_ref[nodes : 2 * nodes, :] = four[...]


def sum_kernel(spread_ref, packed_in, packed_ref):
    acc = spread_ref[0].astype(jnp.float32)
    for c in range(1, spread_ref.shape[0]):
        acc = acc + spread_ref[c].astype(jnp.float32)
    rows = packed_in.shape[0]
    packed_ref[0:rows, :] = packed_in[...]
    packed_ref[rows:, :] = acc.astype(jnp.bfloat16)


def panel_part_kernel(near, four, got_2, got_3, out_ref):
    at = 0
    for part in (near, four, got_2, got_3):
        out_ref[at : at + part.shape[0], :] = part[...]
        at += part.shape[0]


def pair_kernel(sent_in, own, other, sent_out, out_ref):
    total = own[...].astype(jnp.float32) + other[...].astype(jnp.float32)
    out_ref[...] = total.astype(jnp.bfloat16)


def tiles_kernel(
    live_ref, row_ref, col_ref, tiles_hbm, parts, got_1, out_hbm,
    tiles, panel, total, done, arrived, written,
):
    size = tiles.shape[1]
    groups = (live_ref[0] + GROUP - 1) // GROUP

    def fetch(g):
        part = pl.ds(g * GROUP, GROUP)
        return pltpu.make_async_copy(tiles_hbm.at[part], tiles.at[part], arrived.at[g])

    for g in range(tiles.shape[0] // GROUP):
        pl.when(g < groups)(fetch(g).start)
    total[...] = jnp.zeros_like(total)
    place = 0
    for part, count in ((parts, parts.shape[0]), (got_1, parts.shape[0] // 3)):
        for k in range(count // size):
            panel[place] = part[k * size : (k + 1) * size, :]
            place += 1

    def group(g, carry):
        fetch(g).wait()
        first = g * GROUP
        terms = []
        for u in range(GROUP):
            terms.append(
                jnp.dot(
                    tiles[first + u], panel[col_ref[first + u]], preferred_element_type=jnp.float32
                )
            )
        for u in range(GROUP):
            r = row_ref[first + u]
            total[r] = total[r] + terms[u]
        return carry

    lax.fori_loop(0, groups, group, 0)
    owners, height = done.shape[0], done.shape[1]
    results = []
    for c in range(owners):
        for k in range(height // size):
            done[c, k * size : (k + 1) * size, :] = total[c * (height // size) + k].astype(
                jnp.bfloat16
            )
        results.append(pltpu.make_async_copy(done.at[c], out_hbm.at[c], written.at[c]))
        results[-1].start()
    for result in results:
        result.wait()


def halves_kernel(half_ref, after_ref, got_ref, keep_ref, send_ref, total):
    owners, height = got_ref.shape[0], got_ref.shape[1]
    for k in range(height // LANES):
        rows = slice(k * LANES, (k + 1) * LANES)
        acc = got_ref[0, rows, :].astype(jnp.float32)
        for c in range(1, owners):
            acc = acc + got_ref[c, rows, :].astype(jnp.float32)
        total[rows, :] = acc
    own = keep_ref.shape[0]
    half = half_ref[0]
    keep_ref[...] = total[pl.ds(pl.multiple_of(half * own, own), own), :]
    send_ref[...] = total[pl.ds(pl.multiple_of((1 - half) * own, own), own), :].astype(jnp.bfloat16)


def share_kernel(own, other, out_ref, after_ref):
    after_ref[...] = jnp.zeros_like(after_ref)
    total = own[...].astype(jnp.float32) + other[...].astype(jnp.float32)
    total = total.astype(jnp.bfloat16)
    for c in range(out_ref.shape[0]):
        out_ref[c] = total


def features_kernel(before_ref, keep_ref, got_ref, features_ref):
    features_ref[...] = (keep_ref[...] + got_ref[...].astype(jnp.float32)).astype(jnp.bfloat16)


def spread_kernel(shares_ref, weight_ref, after_ref):
    after_ref[...] = jnp.zeros_like(after_ref)
    owners, rows = shares_ref.shape[0], shares_ref.shape[1]
    feats = weight_ref.shape[0]
    for g in range(owners * rows // feats):
        c, at = g * feats // rows, g * feats % rows
        weight_ref[:, g * LANES : (g + 1) * LANES] = shares_ref[c, at : at + feats, :].astype(
            jnp.float32
        )


def shards(grad_out, relu_mask, aggregated, weight, adj_tiles, tile_row, tile_col, tile_count):
    n_row, n_col = lax.axis_size("row"), lax.axis_size("col")
    n_y = n_col // PAIR
    lines = [[y * PAIR + h for y in range(n_y)] for h in range(PAIR)]
    nodes, width = grad_out.shape
    feats = weight.shape[0]
    tile_data = adj_tiles[0, 0]
    slots, size = tile_data.shape[0], tile_data.shape[1]
    block_tiles = nodes * n_col // size
    per_owner = nodes // size
    bf, f32 = jnp.bfloat16, jnp.float32
    shape = jax.ShapeDtypeStruct
    token = shape((8, LANES), f32)

    def swap(value, mask):
        return lax.ppermute(value, "row", [(i, i ^ mask) for i in range(n_row)])

    def swap_pair(value):
        return lax.ppermute(value, "col", [(i, i ^ 1) for i in range(n_col)])

    def line_all_to_all(value):
        return lax.all_to_all(value, "col", 0, 0, axis_index_groups=lines, tiled=True)

    near, first = pl.pallas_call(
        panel_kernel,
        out_shape=(shape((nodes, feats), bf), token),
        in_specs=[HBM] * 3,
        out_specs=(VMEM, VMEM),
        scratch_shapes=[
            pltpu.VMEM((nodes, width), bf),
            pltpu.VMEM((nodes, width), jnp.int32),
            pltpu.VMEM((feats, width), bf),
            pltpu.SemaphoreType.DMA((3,)),
        ],
        compiler_params=params(53.75),
        cost_estimate=cost(2 * nodes * width * feats, nodes * width * 8),
    )(grad_out, relu_mask, weight)

    four = swap(near, 4)

    term, ready = pl.pallas_call(
        weight_kernel,
        out_shape=(shape((width // LANES * feats, LANES), bf), token),
        in_specs=[HBM] * 3 + [VMEM],
        out_specs=(VMEM, VMEM),
        scratch_shapes=[
            pltpu.VMEM((nodes, width), bf),
            pltpu.VMEM((nodes, width), jnp.int32),
            pltpu.VMEM((nodes, feats), bf),
            pltpu.SemaphoreType.DMA((3,)),
        ],
        compiler_params=params(53.9),
        cost_estimate=cost(2 * 10**10, nodes * width * 4),
    )(grad_out, relu_mask, aggregated, first)
    spread = line_all_to_all(term.reshape(n_y, term.shape[0] // n_y, LANES))
    extra = spread.shape[1]
    packed = pl.pallas_call(
        pack_kernel,
        out_shape=shape((2 * nodes, feats), bf),
        in_specs=[VMEM] * 3,
        out_specs=VMEM,
        compiler_params=params(16),
        cost_estimate=cost(2 * 10**10, nodes * feats * 8),
    )(ready, near, four)
    got_2, got_3 = swap(packed, 2), swap(packed, 3)
    loaded = pl.pallas_call(
        sum_kernel,
        out_shape=shape((2 * nodes + extra, LANES), bf),
        in_specs=[VMEM] * 2,
        out_specs=VMEM,
        compiler_params=params(16),
        cost_estimate=cost(2 * 10**10, n_y * extra * LANES * 2),
    )(spread, packed)
    got_1 = swap(loaded, 1)
    parts = pl.pallas_call(
        panel_part_kernel,
        out_shape=shape((6 * nodes, feats), bf),
        in_specs=[VMEM] * 4,
        out_specs=VMEM,
        compiler_params=params(16),
        cost_estimate=cost(2 * 10**10, 12 * nodes * feats * 2),
    )(near, four, got_2, got_3)
    share = loaded[2 * nodes :].astype(f32) + got_1[2 * nodes :].astype(f32)
    share = share.astype(bf)
    row_2 = swap(share, 2)

    live = tile_count[0, 0]
    away = (tile_col[0, 0] * size // nodes) ^ lax.axis_index("row")
    low = away & 3
    slot = jnp.where(low == 0, 0, jnp.where(low == 1, 3, low - 1))
    chunk = slot * 2 + (away >> 2)
    col_at = chunk * per_owner + tile_col[0, 0] % per_owner
    row_at = jnp.where(jnp.arange(slots, dtype=jnp.int32) < live, tile_row[0, 0], block_tiles)

    sent = pl.pallas_call(
        tiles_kernel,
        out_shape=shape((n_y, PAIR * nodes, feats), bf),
        in_specs=[SMEM] * 3 + [HBM] + [VMEM] * 2,
        out_specs=HBM,
        scratch_shapes=[
            pltpu.VMEM((slots, size, size), bf),
            pltpu.VMEM((n_row * per_owner, size, feats), bf),
            pltpu.VMEM((block_tiles + 1, size, feats), f32),
            pltpu.VMEM((n_y, PAIR * nodes, feats), bf),
            pltpu.SemaphoreType.DMA((slots // GROUP,)),
            pltpu.SemaphoreType.DMA((n_y,)),
        ],
        compiler_params=params(50),
        cost_estimate=cost(2 * 10**10, slots * size * size * 2),
    )(live.reshape(1), row_at, col_at, tile_data, parts, got_1)
    sent, share = pl.pallas_call(
        pair_kernel,
        out_shape=(shape(sent.shape, bf), shape((extra, LANES), bf)),
        in_specs=[HBM] + [VMEM] * 2,
        out_specs=(HBM, VMEM),
        input_output_aliases={0: 0},
        compiler_params=params(16),
        cost_estimate=cost(4 * extra * LANES, 4 * extra * LANES * 2),
    )(sent, share, row_2)
    got = line_all_to_all(sent)
    share = (share.astype(f32) + swap(share, 4).astype(f32)).astype(bf)
    far = swap_pair(share)

    whole, ready = pl.pallas_call(
        share_kernel,
        out_shape=(shape((n_y, extra, LANES), bf), token),
        in_specs=[VMEM] * 2,
        out_specs=(VMEM, VMEM),
        compiler_params=params(16),
        cost_estimate=cost(n_y * extra * LANES, n_y * extra * LANES * 2),
    )(share, far)
    shares = line_all_to_all(whole)
    half = (lax.axis_index("col") & (PAIR - 1)).astype(jnp.int32).reshape(1)
    keep, send = pl.pallas_call(
        halves_kernel,
        out_shape=(shape((nodes, feats), f32), shape((nodes, feats), bf)),
        in_specs=[SMEM, HBM, VMEM],
        out_specs=(VMEM, VMEM),
        scratch_shapes=[pltpu.VMEM((PAIR * nodes, feats), f32)],
        compiler_params=params(16),
        cost_estimate=cost(nodes * feats * n_col, nodes * feats * n_col * 2),
    )(half, ready, got)
    other = swap_pair(send)
    grad_weight, after = pl.pallas_call(
        spread_kernel,
        out_shape=(shape((feats, width), f32), token),
        in_specs=[VMEM],
        out_specs=(VMEM, VMEM),
        compiler_params=params(16),
        cost_estimate=cost(feats * width, feats * width * 6),
    )(shares)
    features = pl.pallas_call(
        features_kernel,
        out_shape=shape((nodes, feats), bf),
        in_specs=[HBM] + [VMEM] * 2,
        out_specs=VMEM,
        compiler_params=params(16),
        cost_estimate=cost(nodes * feats, nodes * feats * 4),
    )(after, keep, other)
    return features, grad_weight


def solution(mesh):
    placed = (
        P(("col", "row"), None),
        P(("col", "row"), None),
        P(("col", "row"), "depth"),
        P("depth", None),
        P("row", "col", None, None, None),
        P("row", "col", None),
        P("row", "col", None),
        P("row", "col"),
    )
    return jax.shard_map(
        shards,
        mesh=mesh,
        in_specs=placed,
        out_specs=(P(("row", "col"), "depth"), P("depth", None)),
        check_vma=False,
    )
```

```python
import jax
import jax.numpy as jnp
from jax import lax
from jax.experimental import pallas as pl
from jax.experimental.pallas import tpu as pltpu
from jax.sharding import PartitionSpec as P

LANES = 128
GROUP = 32
PAIR = 2
VMEM = pl.BlockSpec(memory_space=pltpu.VMEM)
SMEM = pl.BlockSpec(memory_space=pltpu.SMEM)
HBM = pl.BlockSpec(memory_space=pl.ANY)


def params(mib):
    return pltpu.CompilerParams(vmem_limit_bytes=int(mib * 2**20))


def cost(flops, moved):
    return pl.CostEstimate(flops=flops, bytes_accessed=moved, transcendentals=0)


def panel_kernel(
    grad_hbm, mask_hbm, weight_hbm, panel_ref, after_ref, grad, mask, weight, arrived
):
    after_ref[...] = jnp.zeros_like(after_ref)
    copies = [
        pltpu.make_async_copy(mask_hbm, mask, arrived.at[0]),
        pltpu.make_async_copy(grad_hbm, grad, arrived.at[1]),
        pltpu.make_async_copy(weight_hbm, weight, arrived.at[2]),
    ]
    for copy in copies:
        copy.start()
    for copy in copies:
        copy.wait()
    masked = grad[...] * mask[...].astype(jnp.float32).astype(jnp.bfloat16)
    panel_ref[...] = lax.dot_general(
        masked, weight[...], (((1,), (1,)), ((), ())), preferred_element_type=jnp.float32
    ).astype(jnp.bfloat16)


def weight_kernel(
    grad_hbm, mask_hbm, aggregated_hbm, before_ref, out_ref, after_ref, grad, mask, aggregated, arrived
):
    copies = [
        pltpu.make_async_copy(mask_hbm, mask, arrived.at[0]),
        pltpu.make_async_copy(grad_hbm, grad, arrived.at[1]),
        pltpu.make_async_copy(aggregated_hbm, aggregated, arrived.at[2]),
    ]
    for copy in copies:
        copy.start()
    for copy in copies:
        copy.wait()
    after_ref[...] = jnp.zeros_like(after_ref)
    flipped = aggregated[...].T
    feats = flipped.shape[0]
    for j in range(grad.shape[1] // LANES):
        part = slice(j * LANES, (j + 1) * LANES)
        masked = grad[:, part] * mask[:, part].astype(jnp.float32).astype(jnp.bfloat16)
        term = jnp.dot(flipped, masked, preferred_element_type=jnp.float32)
        out_ref[j * feats : (j + 1) * feats, :] = term.astype(jnp.bfloat16)


def pack_kernel(after_ref, near, four, packed_ref):
    nodes = near.shape[0]
    packed_ref[0:nodes, :] = near[...]
    packed_ref[nodes : 2 * nodes, :] = four[...]


def sum_kernel(spread_ref, packed_in, packed_ref):
    acc = spread_ref[0].astype(jnp.float32)
    for c in range(1, spread_ref.shape[0]):
        acc = acc + spread_ref[c].astype(jnp.float32)
    rows = packed_in.shape[0]
    packed_ref[0:rows, :] = packed_in[...]
    packed_ref[rows:, :] = acc.astype(jnp.bfloat16)


def panel_part_kernel(near, four, got_2, got_3, out_ref):
    at = 0
    for part in (near, four, got_2, got_3):
        out_ref[at : at + part.shape[0], :] = part[...]
        at += part.shape[0]


def pair_kernel(sent_in, own, other, sent_out, out_ref):
    total = own[...].astype(jnp.float32) + other[...].astype(jnp.float32)
    out_ref[...] = total.astype(jnp.bfloat16)


def tiles_kernel(
    live_ref, row_ref, col_ref, tiles_hbm, parts, got_1, out_hbm,
    tiles, panel, total, done, arrived, written,
):
    size = tiles.shape[1]
    groups = (live_ref[0] + GROUP - 1) // GROUP

    def fetch(g):
        part = pl.ds(g * GROUP, GROUP)
        return pltpu.make_async_copy(tiles_hbm.at[part], tiles.at[part], arrived.at[g])

    for g in range(tiles.shape[0] // GROUP):
        pl.when(g < groups)(fetch(g).start)
    total[...] = jnp.zeros_like(total)
    place = 0
    for part, count in ((parts, parts.shape[0]), (got_1, parts.shape[0] // 3)):
        for k in range(count // size):
            panel[place] = part[k * size : (k + 1) * size, :]
            place += 1

    def group(g, carry):
        fetch(g).wait()
        first = g * GROUP
        terms = []
        for u in range(GROUP):
            terms.append(
                jnp.dot(
                    tiles[first + u], panel[col_ref[first + u]], preferred_element_type=jnp.float32
                )
            )
        for u in range(GROUP):
            r = row_ref[first + u]
            total[r] = total[r] + terms[u]
        return carry

    lax.fori_loop(0, groups, group, 0)
    owners, height = done.shape[0], done.shape[1]
    results = []
    for c in range(owners):
        for k in range(height // size):
            done[c, k * size : (k + 1) * size, :] = total[c * (height // size) + k].astype(
                jnp.bfloat16
            )
        results.append(pltpu.make_async_copy(done.at[c], out_hbm.at[c], written.at[c]))
        results[-1].start()
    for result in results:
        result.wait()


def halves_kernel(half_ref, after_ref, got_ref, keep_ref, send_ref, total):
    owners, height = got_ref.shape[0], got_ref.shape[1]
    for k in range(height // LANES):
        rows = slice(k * LANES, (k + 1) * LANES)
        acc = got_ref[0, rows, :].astype(jnp.float32)
        for c in range(1, owners):
            acc = acc + got_ref[c, rows, :].astype(jnp.float32)
        total[rows, :] = acc
    own = keep_ref.shape[0]
    half = half_ref[0]
    keep_ref[...] = total[pl.ds(pl.multiple_of(half * own, own), own), :]
    send_ref[...] = total[pl.ds(pl.multiple_of((1 - half) * own, own), own), :].astype(jnp.bfloat16)


def share_kernel(own, other, out_ref, after_ref):
    after_ref[...] = jnp.zeros_like(after_ref)
    total = own[...].astype(jnp.float32) + other[...].astype(jnp.float32)
    total = total.astype(jnp.bfloat16)
    for c in range(out_ref.shape[0]):
        out_ref[c] = total


def features_kernel(before_ref, keep_ref, got_ref, features_ref):
    features_ref[...] = (keep_ref[...] + got_ref[...].astype(jnp.float32)).astype(jnp.bfloat16)


def spread_kernel(shares_ref, weight_ref, after_ref):
    after_ref[...] = jnp.zeros_like(after_ref)
    owners, rows = shares_ref.shape[0], shares_ref.shape[1]
    feats = weight_ref.shape[0]
    for g in range(owners * rows // feats):
        c, at = g * feats // rows, g * feats % rows
        weight_ref[:, g * LANES : (g + 1) * LANES] = shares_ref[c, at : at + feats, :].astype(
            jnp.float32
        )


def shards(grad_out, relu_mask, aggregated, weight, adj_tiles, tile_row, tile_col, tile_count):
    n_row, n_col = lax.axis_size("row"), lax.axis_size("col")
    n_y = n_col // PAIR
    lines = [[y * PAIR + h for y in range(n_y)] for h in range(PAIR)]
    nodes, width = grad_out.shape
    feats = weight.shape[0]
    tile_data = adj_tiles[0, 0]
    slots, size = tile_data.shape[0], tile_data.shape[1]
    block_tiles = nodes * n_col // size
    per_owner = nodes // size
    bf, f32 = jnp.bfloat16, jnp.float32
    shape = jax.ShapeDtypeStruct
    token = shape((8, LANES), f32)

    def swap(value, mask):
        return lax.ppermute(value, "row", [(i, i ^ mask) for i in range(n_row)])

    def swap_pair(value):
        return lax.ppermute(value, "col", [(i, i ^ 1) for i in range(n_col)])

    def line_all_to_all(value):
        return lax.all_to_all(value, "col", 0, 0, axis_index_groups=lines, tiled=True)

    near, first = pl.pallas_call(
        panel_kernel,
        out_shape=(shape((nodes, feats), bf), token),
        in_specs=[HBM] * 3,
        out_specs=(VMEM, VMEM),
        scratch_shapes=[
            pltpu.VMEM((nodes, width), bf),
            pltpu.VMEM((nodes, width), jnp.int32),
            pltpu.VMEM((feats, width), bf),
            pltpu.SemaphoreType.DMA((3,)),
        ],
        compiler_params=params(53.75),
        cost_estimate=cost(2 * nodes * width * feats, nodes * width * 8),
    )(grad_out, relu_mask, weight)

    four = swap(near, 4)

    term, ready = pl.pallas_call(
        weight_kernel,
        out_shape=(shape((width // LANES * feats, LANES), bf), token),
        in_specs=[HBM] * 3 + [VMEM],
        out_specs=(VMEM, VMEM),
        scratch_shapes=[
            pltpu.VMEM((nodes, width), bf),
            pltpu.VMEM((nodes, width), jnp.int32),
            pltpu.VMEM((nodes, feats), bf),
            pltpu.SemaphoreType.DMA((3,)),
        ],
        compiler_params=params(53.9),
        cost_estimate=cost(2 * 10**10, nodes * width * 4),
    )(grad_out, relu_mask, aggregated, first)
    spread = line_all_to_all(term.reshape(n_y, term.shape[0] // n_y, LANES))
    extra = spread.shape[1]
    packed = pl.pallas_call(
        pack_kernel,
        out_shape=shape((2 * nodes, feats), bf),
        in_specs=[VMEM] * 3,
        out_specs=VMEM,
        compiler_params=params(16),
        cost_estimate=cost(2 * 10**10, nodes * feats * 8),
    )(ready, near, four)
    got_2, got_3 = swap(packed, 2), swap(packed, 3)
    loaded = pl.pallas_call(
        sum_kernel,
        out_shape=shape((2 * nodes + extra, LANES), bf),
        in_specs=[VMEM] * 2,
        out_specs=VMEM,
        compiler_params=params(16),
        cost_estimate=cost(2 * 10**10, n_y * extra * LANES * 2),
    )(spread, packed)
    got_1 = swap(loaded, 1)
    parts = pl.pallas_call(
        panel_part_kernel,
        out_shape=shape((6 * nodes, feats), bf),
        in_specs=[VMEM] * 4,
        out_specs=VMEM,
        compiler_params=params(16),
        cost_estimate=cost(2 * 10**10, 12 * nodes * feats * 2),
    )(near, four, got_2, got_3)
    share = loaded[2 * nodes :].astype(f32) + got_1[2 * nodes :].astype(f32)
    share = share.astype(bf)
    row_2 = swap(share, 2)

    live = tile_count[0, 0]
    away = (tile_col[0, 0] * size // nodes) ^ lax.axis_index("row")
    low = away & 3
    slot = jnp.where(low == 0, 0, jnp.where(low == 1, 3, low - 1))
    chunk = slot * 2 + (away >> 2)
    col_at = chunk * per_owner + tile_col[0, 0] % per_owner
    row_at = jnp.where(jnp.arange(slots, dtype=jnp.int32) < live, tile_row[0, 0], block_tiles)

    sent = pl.pallas_call(
        tiles_kernel,
        out_shape=shape((n_y, PAIR * nodes, feats), bf),
        in_specs=[SMEM] * 3 + [HBM] + [VMEM] * 2,
        out_specs=HBM,
        scratch_shapes=[
            pltpu.VMEM((slots, size, size), bf),
            pltpu.VMEM((n_row * per_owner, size, feats), bf),
            pltpu.VMEM((block_tiles + 1, size, feats), f32),
            pltpu.VMEM((n_y, PAIR * nodes, feats), bf),
            pltpu.SemaphoreType.DMA((slots // GROUP,)),
            pltpu.SemaphoreType.DMA((n_y,)),
        ],
        compiler_params=params(50),
        cost_estimate=cost(2 * 10**10, slots * size * size * 2),
    )(live.reshape(1), row_at, col_at, tile_data, parts, got_1)
    sent, share = pl.pallas_call(
        pair_kernel,
        out_shape=(shape(sent.shape, bf), shape((extra, LANES), bf)),
        in_specs=[HBM] + [VMEM] * 2,
        out_specs=(HBM, VMEM),
        input_output_aliases={0: 0},
        compiler_params=params(16),
        cost_estimate=cost(4 * extra * LANES, 4 * extra * LANES * 2),
    )(sent, share, row_2)
    got = line_all_to_all(sent)
    share = (share.astype(f32) + swap_pair(share).astype(f32)).astype(bf)
    far = swap(share, 4)

    whole, ready = pl.pallas_call(
        share_kernel,
        out_shape=(shape((n_y, extra, LANES), bf), token),
        in_specs=[VMEM] * 2,
        out_specs=(VMEM, VMEM),
        compiler_params=params(16),
        cost_estimate=cost(n_y * extra * LANES, n_y * extra * LANES * 2),
    )(share, far)
    shares = line_all_to_all(whole)
    half = (lax.axis_index("col") & (PAIR - 1)).astype(jnp.int32).reshape(1)
    keep, send = pl.pallas_call(
        halves_kernel,
        out_shape=(shape((nodes, feats), f32), shape((nodes, feats), bf)),
        in_specs=[SMEM, HBM, VMEM],
        out_specs=(VMEM, VMEM),
        scratch_shapes=[pltpu.VMEM((PAIR * nodes, feats), f32)],
        compiler_params=params(16),
        cost_estimate=cost(nodes * feats * n_col, nodes * feats * n_col * 2),
    )(half, ready, got)
    other = swap_pair(send)
    grad_weight, after = pl.pallas_call(
        spread_kernel,
        out_shape=(shape((feats, width), f32), token),
        in_specs=[VMEM],
        out_specs=(VMEM, VMEM),
        compiler_params=params(16),
        cost_estimate=cost(feats * width, feats * width * 6),
    )(shares)
    features = pl.pallas_call(
        features_kernel,
        out_shape=shape((nodes, feats), bf),
        in_specs=[HBM] + [VMEM] * 2,
        out_specs=VMEM,
        compiler_params=params(16),
        cost_estimate=cost(nodes * feats, nodes * feats * 4),
    )(after, keep, other)
    return features, grad_weight


def solution(mesh):
    placed = (
        P(("col", "row"), None),
        P(("col", "row"), None),
        P(("col", "row"), "depth"),
        P("depth", None),
        P("row", "col", None, None, None),
        P("row", "col", None),
        P("row", "col", None),
        P("row", "col"),
    )
    return jax.shard_map(
        shards,
        mesh=mesh,
        in_specs=placed,
        out_specs=(P(("row", "col"), "depth"), P("depth", None)),
        check_vma=False,
    )
```
